256 devices in a mesh: pipe: 8 (over y_hi, x), fsdp: 32 (over y_lo, z, core).
Axes of the slice: x: 4, y: 4 (y_hi: 2, y_lo: 2; y = y_hi * 2 + y_lo), z: 8, core: 2. Of those that a mesh axis runs over, the one named last changes fastest.
Arguments:
- inputs: bfloat16 [8, 768, 4096], P(None, 'fsdp'), may hold values from -6 to 6
- gains: float32 [16, 4096], P('pipe'), may hold values from 0.25 to 1.75
- proj_gate: bfloat16 [16, 4096, 512], P('pipe', 'fsdp'), may hold values from -0.09375 to 0.09375
- proj_in: bfloat16 [16, 4096, 512], P('pipe', 'fsdp'), may hold values from -0.09375 to 0.09375
- proj_out: bfloat16 [16, 512, 4096], P('pipe', None, 'fsdp'), may hold values from -0.25 to 0.25
- plan: int32 [8], replicated, may hold values from 0 to 7, each once
Outputs:
- finished: bfloat16 [8, 768, 4096], P('pipe', 'fsdp')
The draws below stay inside these ranges and needn't reach their ends.
Inputs may be any that keep to these rules, and one draw needn't show every extreme that they name: `plan`: each slot names a different micro-batch.
All inputs are finite; a program needn't handle non-finite values.
Results may differ from the reference program's by a relative error of at most 0.039.
Values may be sent and summed in bfloat16 or wider, within the bound.
A program may use at most 128 MiB of HBM per device.

```python
import jax
import jax.numpy as jnp
from jax import lax

D = 4096
H = 512
MB = 8
ROWS = 768
BLOCKS = 16


def steps_of(stream_key, dims, pieces, smallest, top_value):
    loudness, own = 1.0, jax.random.fold_in(stream_key, 6)
    for position, parts in pieces:
        heights = jnp.exp(jax.random.uniform(jax.random.fold_in(own, position), (parts,), jnp.float32, smallest / len(pieces), top_value / len(pieces)))
        loudness = loudness * jnp.repeat(heights, dims[position] // parts).reshape([-1 if axis == position else 1 for axis in range(len(dims))])
    return loudness


def scatter_about(key, extent, scale, most, shards=(), dtype=jnp.bfloat16):
    values = scale * jax.random.normal(key, extent, jnp.float32)
    if shards:
        values = values * steps_of(key, extent, shards, -0.22, 0.18)
    return jnp.clip(values, -most, most).astype(dtype)


def setup_inputs(seed: int = 0) -> dict:
    keys = jax.random.split(jax.random.key(seed), 7)
    inputs = scatter_about(keys[0], (MB, ROWS, D), 1.0, 6.0, ((1, 32),))
    gains = jnp.clip(1.0 + 0.15 * jax.random.normal(keys[1], (BLOCKS, D), jnp.float32), 0.25, 1.75)
    proj_gate = scatter_about(keys[2], (BLOCKS, D, H), D ** -0.5, 0.09375, ((0, 8), (1, 32)))
    proj_in = scatter_about(keys[3], (BLOCKS, D, H), D ** -0.5, 0.09375, ((0, 8), (1, 32)))
    proj_out = scatter_about(keys[4], (BLOCKS, H, D), H ** -0.5, 0.25, ((0, 8), (2, 32)))
    plan = jax.random.permutation(keys[5], MB).astype(jnp.int32)
    return {"inputs": inputs, "gains": gains, "proj_gate": proj_gate, "proj_in": proj_in, "proj_out": proj_out, "plan": plan}


def advance(state, gain, w_gate, w_first, w_second):
    wide = state.astype(jnp.float32)
    scale = lax.rsqrt(lax.optimization_barrier(jnp.mean(wide * wide, axis=-1, keepdims=True)) + 1e-05)
    normed = (wide * scale * gain).astype(jnp.bfloat16)
    gated = jax.nn.silu(jnp.dot(normed, w_gate, preferred_element_type=jnp.float32))
    hidden = (gated * jnp.dot(normed, w_first, preferred_element_type=jnp.float32)).astype(jnp.bfloat16)
    return (wide + jnp.dot(hidden, w_second, preferred_element_type=jnp.float32)).astype(jnp.bfloat16)

def reference(inputs, gains, proj_gate, proj_in, proj_out, plan):
    ordered = jnp.take(inputs, plan.astype(jnp.int32), axis=0)

    def run_slot(state):
        for block in range(BLOCKS):
            stored = 2 * (block % MB) + block // MB
            state = advance(state, gains[stored], proj_gate[stored], proj_in[stored], proj_out[stored])
        return state
    return lax.map(run_slot, ordered)
```

```python
import functools

import jax
import jax.numpy as jnp
from jax import lax
from jax.experimental import pallas as pl
from jax.experimental.pallas import tpu as pltpu
from jax.sharding import PartitionSpec as P

MESH = pl.DeviceIdType.MESH
PIPE, FSDP, ZN = 8, 32, 8
D, H, SLICE = 4096, 512, 128
LAPS, MB, TOK = 2, 8, 24
GROUP = 16
GROUPS = MB * TOK // GROUP
CHUNKS = 4
CW = D // CHUNKS
STEPS, LINKS, KINDS = 5, 3, 3
EPS = 1e-05


def kernel(
    plan_ref,
    inputs_ref,
    gains_ref,
    gate_ref,
    first_ref,
    second_ref,
    o_ref,
    w_gate,
    w_first,
    w_second,
    staged,
    xbuf,
    landing,
    stage_sem,
    own_sem,
    gather_send,
    gather_recv,
    pair_send,
    pair_recv,
    x_send,
    x_recv,
    end_send,
    end_recv,
):
    p = lax.axis_index("pipe")
    f = lax.axis_index("fsdp")
    y = f // 16
    z = (f // 2) % ZN
    core = f % 2

    def shard(other, dz):
        row = 1 - y if other else y
        return row * 16 + ((z + dz + ZN) % ZN) * 2 + core

    up, down, across = (p, shard(0, 1)), (p, shard(0, -1)), (p, shard(1, 0))
    twin = (p, f + 1 - 2 * core)
    targets = (up, down, across)

    barrier = pltpu.get_barrier_semaphore()
    for device in (up, down, across, twin):
        pl.semaphore_signal(barrier, inc=1, device_id=device, device_id_type=MESH)
    for ahead in range(1, PIPE):
        pl.semaphore_signal(
            barrier, inc=1, device_id=((p + ahead) % PIPE, f), device_id_type=MESH
        )
    pl.semaphore_wait(barrier, 4 + PIPE - 1)

    sends = (
        ((0, 0), (0, -1), (0, -2), (0, -3), (1, -3)),
        ((0, 0), (0, 1), (0, 2), (1, 0), (1, 1)),
        ((0, 0), (0, -1), (0, -2), (0, -3), (0, 3)),
    )
    gets = (
        ((0, -1), (0, -2), (0, -3), (0, -4), (1, -4)),
        ((0, 1), (0, 2), (0, 3), (1, 1), (1, 2)),
        ((1, 0), (1, -1), (1, -2), (1, -3), (1, 3)),
    )

    def place(kind, lap, index):
        part = pl.ds(pl.multiple_of(index * SLICE, SLICE), SLICE)
        if kind == 0:
            return w_gate.at[lap, part, :]
        if kind == 1:
            return w_first.at[lap, part, :]
        return w_second.at[lap, :, part]

    def own(kind, lap):
        return (gate_ref, first_ref, second_ref)[kind].at[lap]

    def bulk(kind, lap, shards):
        if kind == 0:
            return w_gate.at[lap, pl.ds(0, shards * SLICE), :]
        if kind == 1:
            return w_first.at[lap, pl.ds(0, shards * SLICE), :]
        return w_second.at[lap, :, pl.ds(0, shards * SLICE)]

    def send(lap, step, kind):
        for link in range(LINKS):
            index = shard(*sends[link][step])
            source = own(kind, lap) if step == 0 else place(kind, lap, index)
            pltpu.make_async_remote_copy(
                src_ref=source,
                dst_ref=place(kind, lap, index),
                send_sem=gather_send.at[lap, link, kind],
                recv_sem=gather_recv.at[lap, link, step, kind],
                device_id=targets[link],
                device_id_type=MESH,
            ).start()

    def to_twin(lap, kind, index, source):
        pltpu.make_async_remote_copy(
            src_ref=source,
            dst_ref=place(kind, lap, index),
            send_sem=pair_send.at[lap, kind],
            recv_sem=pair_recv.at[lap, kind],
            device_id=twin,
            device_id_type=MESH,
        ).start()

    def keep_own(lap, kind):
        return pltpu.make_async_copy(own(kind, lap), place(kind, lap, f), own_sem.at[lap, kind])

    def gather_begin(lap):
        for kind in range(KINDS):
            send(lap, 0, kind)
        for kind in range(KINDS):
            to_twin(lap, kind, f, own(kind, lap))
            keep_own(lap, kind).start()

    def gather_step(lap, step, kind):
        for link in range(LINKS):
            target = place(kind, lap, shard(*gets[link][step]))
            pltpu.make_async_remote_copy(
                src_ref=target,
                dst_ref=target,
                send_sem=gather_send.at[lap, link, kind],
                recv_sem=gather_recv.at[lap, link, step, kind],
                device_id=targets[link],
                device_id_type=MESH,
            ).wait_recv()
        if step + 1 < STEPS:
            send(lap, step + 1, kind)
        for link in range(LINKS):
            index = shard(*gets[link][step])
            to_twin(lap, kind, index, place(kind, lap, index))

    def gather_end(lap):
        for kind in range(KINDS):
            whole = bulk(kind, lap, 16)
            pltpu.make_async_remote_copy(
                src_ref=whole,
                dst_ref=whole,
                send_sem=pair_send.at[lap, kind],
                recv_sem=pair_recv.at[lap, kind],
                device_id=twin,
                device_id_type=MESH,
            ).wait_recv()
            keep_own(lap, kind).wait()

    def gather_drain(lap):
        for kind in range(KINDS):
            for link in range(LINKS):
                part = bulk(kind, lap, STEPS)
                pltpu.make_async_remote_copy(
                    src_ref=part,
                    dst_ref=part,
                    send_sem=gather_send.at[lap, link, kind],
                    recv_sem=gather_recv.at[lap, link, 0, kind],
                    device_id=targets[link],
                    device_id_type=MESH,
                ).wait_send()
            whole = bulk(kind, lap, 16)
            pltpu.make_async_remote_copy(
                src_ref=whole,
                dst_ref=whole,
                send_sem=pair_send.at[lap, kind],
                recv_sem=pair_recv.at[lap, kind],
                device_id=twin,
                device_id_type=MESH,
            ).wait_send()

    order = [(step, kind) for step in range(STEPS) for kind in range(KINDS)]

    gather_begin(0)

    @pl.when(p == 0)
    def _():
        stage = pltpu.make_async_copy(inputs_ref, staged, stage_sem)
        stage.start()
        stage.wait()
        for pair in range(MB // 2):
            even = staged[plan_ref[2 * pair]].astype(jnp.float32)
            odd = staged[plan_ref[2 * pair + 1]].astype(jnp.float32)
            xbuf[0, 3 * pair] = even[:16].astype(jnp.bfloat16)
            xbuf[0, 3 * pair + 1] = jnp.concatenate([even[16:], odd[:8]], axis=0).astype(
                jnp.bfloat16
            )
            xbuf[0, 3 * pair + 2] = odd[8:].astype(jnp.bfloat16)

    for step, kind in order:
        gather_step(0, step, kind)
    gather_begin(1)
    gather_end(0)

    onward = ((p + 1) % PIPE, f)

    def columns(chunk):
        return pl.ds(chunk * CW, CW)

    def hop(lap, group, chunk, to_lap):
        return pltpu.make_async_remote_copy(
            src_ref=xbuf.at[lap, group, :, columns(chunk)],
            dst_ref=xbuf.at[to_lap, group, :, columns(chunk)],
            send_sem=x_send.at[lap, group],
            recv_sem=x_recv.at[to_lap, group, chunk],
            device_id=onward,
            device_id_type=MESH,
        )

    def finish(group, second, slot):
        return pltpu.make_async_remote_copy(
            src_ref=xbuf.at[1, group],
            dst_ref=landing.at[1 - second if second else jnp.where(group % 3 == 0, 0, 1)],
            send_sem=end_send.at[second, group],
            recv_sem=end_recv.at[1 - second if second else jnp.where(group % 3 == 0, 0, 1)],
            device_id=(slot, f),
            device_id_type=MESH,
        )

    def slots(group):
        pair = group // 3
        return 2 * pair + jnp.where(group % 3 == 2, 1, 0), 2 * pair + 1

    def one(turn, carry):
        lap = turn // GROUPS
        group = turn % GROUPS
        for number in range(GROUPS):
            @pl.when(turn == number)
            def _():
                gather_step(1, *order[number])

        @pl.when(turn == GROUPS)
        def _():
            for step, kind in order[GROUPS:]:
                gather_step(1, step, kind)
            gather_end(1)

        total_gate = jnp.zeros((GROUP, H), jnp.float32)
        total_first = jnp.zeros((GROUP, H), jnp.float32)
        squares = jnp.zeros((GROUP, 1), jnp.float32)
        for chunk in range(CHUNKS):
            @pl.when((p > 0) | (lap > 0))
            def _():
                hop(lap, group, chunk, lap).wait_recv()

            wide = xbuf[lap, group, :, columns(chunk)].astype(jnp.float32)
            squares += jnp.sum(wide * wide, axis=-1, keepdims=True)
            scaled = (wide * gains_ref[pl.ds(lap, 1), columns(chunk)]).astype(jnp.bfloat16)
            total_gate += jnp.dot(
                scaled, w_gate[lap, columns(chunk), :], preferred_element_type=jnp.float32
            )
            total_first += jnp.dot(
                scaled, w_first[lap, columns(chunk), :], preferred_element_type=jnp.float32
            )
        scale = lax.rsqrt(squares * (1.0 / D) + EPS)
        gate = total_gate * scale
        hidden = (gate / (1.0 + jnp.exp(-gate)) * (total_first * scale)).astype(jnp.bfloat16)
        last = (p == PIPE - 1) & (lap == 1)
        to_lap = jnp.where(p == PIPE - 1, 1, lap)
        for chunk in range(CHUNKS):
            wide = xbuf[lap, group, :, columns(chunk)].astype(jnp.float32)
            wide += jnp.dot(
                hidden, w_second[lap, :, columns(chunk)], preferred_element_type=jnp.float32
            )
            xbuf[lap, group, :, columns(chunk)] = wide.astype(jnp.bfloat16)

            @pl.when(jnp.logical_not(last))
            def _():
                hop(lap, group, chunk, to_lap).start()

        slot, after = slots(group)

        @pl.when(last & (group < GROUPS - 1))
        def _():
            finish(group, 0, slot).start()

        @pl.when(last & (group % 3 == 1) & (group < GROUPS - 2))
        def _():
            finish(group, 1, after).start()

        return carry

    lax.fori_loop(0, LAPS * GROUPS, one, 0)

    def put(head, tail):
        head, tail = head.astype(jnp.float32), tail.astype(jnp.float32)

        @pl.when(p % 2 == 0)
        def _():
            o_ref[0] = jnp.concatenate([head, tail[:8]], axis=0).astype(jnp.bfloat16)

        @pl.when(p % 2 == 1)
        def _():
            o_ref[0] = jnp.concatenate([head[8:], tail], axis=0).astype(jnp.bfloat16)

    @pl.when(p < PIPE - 1)
    def _():
        for place_in in range(2):
            pltpu.make_async_remote_copy(
                src_ref=landing.at[place_in],
                dst_ref=landing.at[place_in],
                send_sem=end_send.at[0, 0],
                recv_sem=end_recv.at[place_in],
                device_id=onward,
                device_id_type=MESH,
            ).wait_recv()
        put(landing[0], landing[1])

    @pl.when(p == PIPE - 1)
    def _():
        put(xbuf[1, GROUPS - 2], xbuf[1, GROUPS - 1])

    for lap in range(LAPS):
        gather_drain(lap)

    def sent(turn, carry):
        lap = turn // GROUPS
        group = turn % GROUPS
        last = (p == PIPE - 1) & (lap == 1)

        @pl.when(jnp.logical_not(last))
        def _():
            pltpu.make_async_remote_copy(
                src_ref=xbuf.at[lap, group],
                dst_ref=xbuf.at[lap, group],
                send_sem=x_send.at[lap, group],
                recv_sem=x_recv.at[lap, group, 0],
                device_id=onward,
                device_id_type=MESH,
            ).wait_send()

        @pl.when(last & (group < GROUPS - 1))
        def _():
            finish(group, 0, 0).wait_send()

        @pl.when(last & (group % 3 == 1) & (group < GROUPS - 2))
        def _():
            finish(group, 1, 0).wait_send()

        return carry

    lax.fori_loop(0, LAPS * GROUPS, sent, 0)


def local(inputs, gains, proj_gate, proj_in, proj_out, plan):
    anywhere = pl.BlockSpec(memory_space=pl.ANY)
    vmem = pl.BlockSpec(memory_space=pltpu.VMEM)
    dma = pltpu.SemaphoreType.DMA
    rows = MB * TOK
    return pl.pallas_call(
        kernel,
        out_shape=jax.ShapeDtypeStruct((1, TOK, D), jnp.bfloat16),
        in_specs=[
            pl.BlockSpec(memory_space=pltpu.SMEM),
            anywhere,
            vmem,
            anywhere,
            anywhere,
            anywhere,
        ],
        out_specs=vmem,
        scratch_shapes=[
            pltpu.VMEM((LAPS, D, H), jnp.bfloat16),
            pltpu.VMEM((LAPS, D, H), jnp.bfloat16),
            pltpu.VMEM((LAPS, H, D), jnp.bfloat16),
            pltpu.VMEM((MB, TOK, D), jnp.bfloat16),
            pltpu.VMEM((LAPS, GROUPS, GROUP, D), jnp.bfloat16),
            pltpu.VMEM((2, GROUP, D), jnp.bfloat16),
            dma,
            dma((LAPS, KINDS)),
            dma((LAPS, LINKS, KINDS)),
            dma((LAPS, LINKS, STEPS, KINDS)),
            dma((LAPS, KINDS)),
            dma((LAPS, KINDS)),
            dma((LAPS, GROUPS)),
            dma((LAPS, GROUPS, CHUNKS)),
            dma((2, GROUPS)),
            dma((2,)),
        ],
        compiler_params=pltpu.CompilerParams(
            collective_id=0, has_side_effects=True, vmem_limit_bytes=56 << 20
        ),
        cost_estimate=pl.CostEstimate(
            flops=LAPS * rows * D * H * 6, bytes_accessed=LAPS * D * H * 6, transcendentals=0
        ),
        name="sections",
    )(plan, inputs, gains, proj_gate, proj_in, proj_out)


def solution(mesh):
    in_specs = (
        P(None, "fsdp", None),
        P("pipe", None),
        P("pipe", "fsdp", None),
        P("pipe", "fsdp", None),
        P("pipe", None, "fsdp"),
        P(),
    )
    out_specs = P("pipe", "fsdp", None)
    return jax.shard_map(local, mesh=mesh, in_specs=in_specs, out_specs=out_specs, check_vma=False)
```

```python
import functools

import jax
import jax.numpy as jnp
from jax import lax
from jax.experimental import pallas as pl
from jax.experimental.pallas import tpu as pltpu
from jax.sharding import PartitionSpec as P

MESH = pl.DeviceIdType.MESH
PIPE, FSDP, ZN = 8, 32, 8
D, H, SLICE = 4096, 512, 128
LAPS, MB, TOK = 2, 8, 24
GROUP = 16
GROUPS = MB * TOK // GROUP
CHUNKS = 4
CW = D // CHUNKS
STEPS, LINKS, KINDS = 5, 3, 3
ROUNDS = STEPS * KINDS
EARLY = 2
EPS = 1e-05


def kernel(
    plan_ref,
    inputs_ref,
    gains_ref,
    gate_ref,
    first_ref,
    second_ref,
    o_ref,
    w_gate,
    w_first,
    w_second,
    staged,
    xbuf,
    landing,
    stage_sem,
    own_sem,
    gather_send,
    gather_recv,
    pair_send,
    pair_recv,
    x_send,
    x_recv,
    end_send,
    end_recv,
):
    p = lax.axis_index("pipe")
    f = lax.axis_index("fsdp")
    y = f // 16
    z = (f // 2) % ZN
    core = f % 2

    def shard(other, dz):
        row = (y + other) % 2
        return row * 16 + ((z + dz + ZN) % ZN) * 2 + core

    up, down, across = (p, shard(0, 1)), (p, shard(0, -1)), (p, shard(1, 0))
    twin = (p, f + 1 - 2 * core)
    targets = (up, down, across)

    barrier = pltpu.get_barrier_semaphore()
    for device in (up, down, across, twin):
        pl.semaphore_signal(barrier, inc=1, device_id=device, device_id_type=MESH)
    for ahead in range(1, PIPE):
        pl.semaphore_signal(
            barrier, inc=1, device_id=((p + ahead) % PIPE, f), device_id_type=MESH
        )
    for ahead in (1, PIPE - 1):
        pl.semaphore_signal(
            barrier,
            inc=1,
            device_id=((p + ahead) % PIPE, shard(1, 0)),
            device_id_type=MESH,
        )
    pl.semaphore_wait(barrier, 4 + PIPE - 1 + 2)

    plan = (
        ((0, 0), (0, -1), (0, -2), (0, -3), (1, -3)),
        ((0, 0), (0, 1), (0, 2), (1, 0), (1, 1)),
        ((0, 0), (0, -1), (0, -2), (0, -3), (0, 3)),
    )
    moves = ((0, -1), (0, 1), (1, 0))

    def pick(link, step, part):
        if isinstance(step, int):
            return plan[link][step][part]
        found = plan[link][0][part]
        for number in range(1, STEPS):
            found = jnp.where(step == number, plan[link][number][part], found)
        return found

    def sent_shard(link, step):
        return shard(pick(link, step, 0), pick(link, step, 1))

    def got_shard(link, step):
        other, dz = moves[link]
        return shard(pick(link, step, 0) + other, pick(link, step, 1) + dz)

    def place(kind, lap, index):
        part = pl.ds(pl.multiple_of(index * SLICE, SLICE), SLICE)
        if kind == 0:
            return w_gate.at[lap, part, :]
        if kind == 1:
            return w_first.at[lap, part, :]
        return w_second.at[lap, :, part]

    def own(kind, lap):
        return (gate_ref, first_ref, second_ref)[kind].at[lap]

    def bulk(kind, lap, shards):
        if kind == 0:
            return w_gate.at[lap, pl.ds(0, shards * SLICE), :]
        if kind == 1:
            return w_first.at[lap, pl.ds(0, shards * SLICE), :]
        return w_second.at[lap, :, pl.ds(0, shards * SLICE)]

    def send(lap, step, kind):
        fresh = isinstance(step, int) and step == 0
        for link in range(LINKS):
            index = f if fresh else sent_shard(link, step)
            pltpu.make_async_remote_copy(
                src_ref=own(kind, lap) if fresh else place(kind, lap, index),
                dst_ref=place(kind, lap, index),
                send_sem=gather_send.at[lap, link, kind],
                recv_sem=gather_recv.at[lap, link, step, kind],
                device_id=targets[link],
                device_id_type=MESH,
            ).start()

    def to_twin(lap, kind, index, source):
        pltpu.make_async_remote_copy(
            src_ref=source,
            dst_ref=place(kind, lap, index),
            send_sem=pair_send.at[lap, kind],
            recv_sem=pair_recv.at[lap, kind],
            device_id=twin,
            device_id_type=MESH,
        ).start()

    def keep_own(lap, kind):
        return pltpu.make_async_copy(own(kind, lap), place(kind, lap, f), own_sem.at[lap, kind])

    def gather_begin(lap):
        for kind in range(KINDS):
            send(lap, 0, kind)
        for kind in range(KINDS):
            to_twin(lap, kind, f, own(kind, lap))
            keep_own(lap, kind).start()

    def gather_step(lap, step, kind):
        for link in range(LINKS):
            target = place(kind, lap, got_shard(link, step))
            pltpu.make_async_remote_copy(
                src_ref=target,
                dst_ref=target,
                send_sem=gather_send.at[lap, link, kind],
                recv_sem=gather_recv.at[lap, link, step, kind],
                device_id=targets[link],
                device_id_type=MESH,
            ).wait_recv()
        if isinstance(step, int):
            if step + 1 < STEPS:
                send(lap, step + 1, kind)
        else:
            pl.when(step + 1 < STEPS)(functools.partial(send, lap, step + 1, kind))
        for link in range(LINKS):
            index = got_shard(link, step)
            to_twin(lap, kind, index, place(kind, lap, index))

    def gather_end(lap, kind):
        whole = bulk(kind, lap, 16)
        pltpu.make_async_remote_copy(
            src_ref=whole,
            dst_ref=whole,
            send_sem=pair_send.at[lap, kind],
            recv_sem=pair_recv.at[lap, kind],
            device_id=twin,
            device_id_type=MESH,
        ).wait_recv()
        keep_own(lap, kind).wait()

    def gather_drain(lap):
        for kind in range(KINDS):
            for link in range(LINKS):
                part = bulk(kind, lap, STEPS)
                pltpu.make_async_remote_copy(
                    src_ref=part,
                    dst_ref=part,
                    send_sem=gather_send.at[lap, link, kind],
                    recv_sem=gather_recv.at[lap, link, 0, kind],
                    device_id=targets[link],
                    device_id_type=MESH,
                ).wait_send()
            whole = bulk(kind, lap, 16)
            pltpu.make_async_remote_copy(
                src_ref=whole,
                dst_ref=whole,
                send_sem=pair_send.at[lap, kind],
                recv_sem=pair_recv.at[lap, kind],
                device_id=twin,
                device_id_type=MESH,
            ).wait_send()

    gather_begin(0)

    @pl.when(p == 0)
    def _():
        stage = pltpu.make_async_copy(inputs_ref, staged, stage_sem)
        stage.start()
        stage.wait()
        for pair in range(MB // 2):
            even = staged[plan_ref[2 * pair]].astype(jnp.float32)
            odd = staged[plan_ref[2 * pair + 1]].astype(jnp.float32)
            xbuf[0, 3 * pair] = even[:16].astype(jnp.bfloat16)
            xbuf[0, 3 * pair + 1] = jnp.concatenate([even[16:], odd[:8]], axis=0).astype(
                jnp.bfloat16
            )
            xbuf[0, 3 * pair + 2] = odd[8:].astype(jnp.bfloat16)

    for step in range(STEPS):
        for kind in range(KINDS):
            gather_step(0, step, kind)
        if step == STEPS - 2:
            gather_begin(1)
    for kind in range(KINDS - 1):
        gather_end(0, kind)

    def next_lap(number, carry):
        for kind in range(KINDS):
            @pl.when(number % KINDS == kind)
            def _():
                gather_step(1, number // KINDS, kind)

        return carry

    early = EARLY * p
    lax.fori_loop(0, early, next_lap, 0)

    onward = ((p + 1) % PIPE, f)
    turned = ((p + 1) % PIPE, shard(1, 0))
    crossing = (p % 4) == 3

    def columns(chunk):
        return pl.ds(chunk * CW, CW)

    def hop(lap, group, chunk, to_lap, device):
        return pltpu.make_async_remote_copy(
            src_ref=xbuf.at[lap, group, :, columns(chunk)],
            dst_ref=xbuf.at[to_lap, group, :, columns(chunk)],
            send_sem=x_send.at[lap, group],
            recv_sem=x_recv.at[to_lap, group, chunk],
            device_id=device,
            device_id_type=MESH,
        )

    def finish(group, second, slot):
        return pltpu.make_async_remote_copy(
            src_ref=xbuf.at[1, group],
            dst_ref=landing.at[1 - second if second else jnp.where(group % 3 == 0, 0, 1)],
            send_sem=end_send.at[second, group],
            recv_sem=end_recv.at[1 - second if second else jnp.where(group % 3 == 0, 0, 1)],
            device_id=(slot, f),
            device_id_type=MESH,
        )

    def slots(group):
        pair = group // 3
        return 2 * pair + jnp.where(group % 3 == 2, 1, 0), 2 * pair + 1

    def one(turn, carry):
        lap = turn // GROUPS
        group = turn % GROUPS
        step = early + turn - 1

        @pl.when((turn > 0) & (turn < GROUPS) & (step < ROUNDS))
        def _():
            next_lap(step, 0)

        @pl.when(turn == GROUPS)
        def _():
            lax.fori_loop(jnp.minimum(step, ROUNDS), ROUNDS, next_lap, 0)
            for kind in range(KINDS):
                gather_end(1, kind)

        total_gate = jnp.zeros((GROUP, H), jnp.float32)
        total_first = jnp.zeros((GROUP, H), jnp.float32)
        squares = jnp.zeros((GROUP, 1), jnp.float32)
        for chunk in range(CHUNKS):
            @pl.when((p > 0) | (lap > 0))
            def _():
                hop(lap, group, chunk, lap, onward).wait_recv()

            wide = xbuf[lap, group, :, columns(chunk)].astype(jnp.float32)
            squares += jnp.sum(wide * wide, axis=-1, keepdims=True)
            scaled = (wide * gains_ref[pl.ds(lap, 1), columns(chunk)]).astype(jnp.bfloat16)
            total_gate += jnp.dot(
                scaled, w_gate[lap, columns(chunk), :], preferred_element_type=jnp.float32
            )
            total_first += jnp.dot(
                scaled, w_first[lap, columns(chunk), :], preferred_element_type=jnp.float32
            )
        scale = lax.rsqrt(squares * (1.0 / D) + EPS)
        gate = total_gate * scale
        hidden = (gate / (1.0 + jnp.exp(-gate)) * (total_first * scale)).astype(jnp.bfloat16)

        @pl.when(turn == 0)
        def _():
            gather_end(0, KINDS - 1)

        last = (p == PIPE - 1) & (lap == 1)
        to_lap = jnp.where(p == PIPE - 1, 1, lap)
        turning = crossing & (lap == 0)
        for chunk in range(CHUNKS):
            wide = xbuf[lap, group, :, columns(chunk)].astype(jnp.float32)
            wide += jnp.dot(
                hidden, w_second[lap, :, columns(chunk)], preferred_element_type=jnp.float32
            )
            xbuf[lap, group, :, columns(chunk)] = wide.astype(jnp.bfloat16)

            @pl.when(jnp.logical_not(last | turning))
            def _():
                hop(lap, group, chunk, to_lap, onward).start()

            @pl.when(turning)
            def _():
                hop(lap, group, chunk, to_lap, turned).start()

        slot, after = slots(group)

        @pl.when(last & (group < GROUPS - 1))
        def _():
            finish(group, 0, slot).start()

        @pl.when(last & (group % 3 == 1) & (group < GROUPS - 2))
        def _():
            finish(group, 1, after).start()

        return carry

    lax.fori_loop(0, LAPS * GROUPS, one, 0)

    def put(head, tail):
        head, tail = head.astype(jnp.float32), tail.astype(jnp.float32)

        @pl.when(p % 2 == 0)
        def _():
            o_ref[0] = jnp.concatenate([head, tail[:8]], axis=0).astype(jnp.bfloat16)

        @pl.when(p % 2 == 1)
        def _():
            o_ref[0] = jnp.concatenate([head[8:], tail], axis=0).astype(jnp.bfloat16)

    @pl.when(p < PIPE - 1)
    def _():
        for place_in in range(2):
            pltpu.make_async_remote_copy(
                src_ref=landing.at[place_in],
                dst_ref=landing.at[place_in],
                send_sem=end_send.at[0, 0],
                recv_sem=end_recv.at[place_in],
                device_id=onward,
                device_id_type=MESH,
            ).wait_recv()
        put(landing[0], landing[1])

    @pl.when(p == PIPE - 1)
    def _():
        put(xbuf[1, GROUPS - 2], xbuf[1, GROUPS - 1])

    for lap in range(LAPS):
        gather_drain(lap)

    def sent(turn, carry):
        lap = turn // GROUPS
        group = turn % GROUPS
        last = (p == PIPE - 1) & (lap == 1)

        @pl.when(jnp.logical_not(last))
        def _():
            pltpu.make_async_remote_copy(
                src_ref=xbuf.at[lap, group],
                dst_ref=xbuf.at[lap, group],
                send_sem=x_send.at[lap, group],
                recv_sem=x_recv.at[lap, group, 0],
                device_id=onward,
                device_id_type=MESH,
            ).wait_send()

        @pl.when(last & (group < GROUPS - 1))
        def _():
            finish(group, 0, 0).wait_send()

        @pl.when(last & (group % 3 == 1) & (group < GROUPS - 2))
        def _():
            finish(group, 1, 0).wait_send()

        return carry

    lax.fori_loop(0, LAPS * GROUPS, sent, 0)


def local(inputs, gains, proj_gate, proj_in, proj_out, plan):
    anywhere = pl.BlockSpec(memory_space=pl.ANY)
    vmem = pl.BlockSpec(memory_space=pltpu.VMEM)
    dma = pltpu.SemaphoreType.DMA
    rows = MB * TOK
    return pl.pallas_call(
        kernel,
        out_shape=jax.ShapeDtypeStruct((1, TOK, D), jnp.bfloat16),
        in_specs=[
            pl.BlockSpec(memory_space=pltpu.SMEM),
            anywhere,
            vmem,
            anywhere,
            anywhere,
            anywhere,
        ],
        out_specs=vmem,
        scratch_shapes=[
            pltpu.VMEM((LAPS, D, H), jnp.bfloat16),
            pltpu.VMEM((LAPS, D, H), jnp.bfloat16),
            pltpu.VMEM((LAPS, H, D), jnp.bfloat16),
            pltpu.VMEM((MB, TOK, D), jnp.bfloat16),
            pltpu.VMEM((LAPS, GROUPS, GROUP, D), jnp.bfloat16),
            pltpu.VMEM((2, GROUP, D), jnp.bfloat16),
            dma,
            dma((LAPS, KINDS)),
            dma((LAPS, LINKS, KINDS)),
            dma((LAPS, LINKS, STEPS, KINDS)),
            dma((LAPS, KINDS)),
            dma((LAPS, KINDS)),
            dma((LAPS, GROUPS)),
            dma((LAPS, GROUPS, CHUNKS)),
            dma((2, GROUPS)),
            dma((2,)),
        ],
        compiler_params=pltpu.CompilerParams(
            collective_id=0, has_side_effects=True, vmem_limit_bytes=56 << 20
        ),
        cost_estimate=pl.CostEstimate(
            flops=LAPS * rows * D * H * 6, bytes_accessed=LAPS * D * H * 6, transcendentals=0
        ),
        name="sections",
    )(plan, inputs, gains, proj_gate, proj_in, proj_out)


def solution(mesh):
    in_specs = (
        P(None, "fsdp", None),
        P("pipe", None),
        P("pipe", "fsdp", None),
        P("pipe", "fsdp", None),
        P("pipe", None, "fsdp"),
        P(),
    )
    out_specs = P("pipe", "fsdp", None)
    return jax.shard_map(local, mesh=mesh, in_specs=in_specs, out_specs=out_specs, check_vma=False)
```

```python
import functools

import jax
import jax.numpy as jnp
from jax import lax
from jax.experimental import pallas as pl
from jax.experimental.pallas import tpu as pltpu
from jax.sharding import PartitionSpec as P

MESH = pl.DeviceIdType.MESH
PIPE, FSDP, ZN = 8, 32, 8
D, H, SLICE = 4096, 512, 128
LAPS, MB, TOK = 2, 8, 24
GROUP = 16
GROUPS = MB * TOK // GROUP
MOVED = 2
MOST = GROUPS + MOVED
CHUNKS = 8
CW = D // CHUNKS
STEPS, LINKS, KINDS = 5, 3, 3
ROUNDS = STEPS * KINDS
EARLY = 2
LATER = 6
RELAYED = 2
EPS = 1e-05


def kernel(
    plan_ref,
    inputs_ref,
    gains_ref,
    gate_ref,
    first_ref,
    second_ref,
    o_ref,
    w_gate,
    w_first,
    w_second,
    staged,
    ordered,
    xbuf,
    landing,
    passing,
    passing_second,
    stage_sem,
    own_sem,
    gather_send,
    gather_recv,
    pair_send,
    pair_recv,
    x_send,
    x_recv,
    end_send,
    end_recv,
    over_send,
    relay_send,
    relay_recv,
):
    p = lax.axis_index("pipe")
    f = lax.axis_index("fsdp")
    y = f // 16
    z = (f // 2) % ZN
    core = f % 2

    def shard(other, dz):
        row = (y + other) % 2
        return row * 16 + ((z + dz + ZN) % ZN) * 2 + core

    up, down, across = (p, shard(0, 1)), (p, shard(0, -1)), (p, shard(1, 0))
    twin = (p, f + 1 - 2 * core)
    targets = (up, down, across)

    barrier = pltpu.get_barrier_semaphore()
    def greet(device):
        pl.semaphore_signal(barrier, inc=1, device_id=device, device_id_type=MESH)

    other = twin[1]
    before, after = (p + PIPE - 1) % PIPE, (p + 1) % PIPE
    for device in (up, down, across, twin):
        greet(device)
    mate = ((p + PIPE // 2) % PIPE, shard(1, 0))
    greet(mate)
    for section in (before, after):
        greet((section, f))
        greet((section, shard(1, 0)))

    @pl.when(p == PIPE - 1)
    def _():
        for section in range(PIPE - 1):
            greet((section, other))
            if 0 < section < PIPE - 2:
                greet((section, f))

    @pl.when(p < PIPE - 1)
    def _():
        greet((PIPE - 1, other))

    @pl.when((p > 0) & (p < PIPE - 2))
    def _():
        greet((PIPE - 1, f))

    @pl.when(p == PIPE - 1)
    def _():
        pl.semaphore_wait(barrier, 9 + 2 * PIPE - 4)

    @pl.when((p > 0) & (p < PIPE - 2))
    def _():
        pl.semaphore_wait(barrier, 9 + 2)

    @pl.when((p == 0) | (p == PIPE - 2))
    def _():
        pl.semaphore_wait(barrier, 9 + 1)

    even = (
        ((0, 0), (0, -1), (0, -2), (0, -3), (1, -3)),
        ((0, 0), (0, 1), (0, 2), (1, 0), (1, 1)),
        ((0, 0), (0, -1), (0, -2), (0, -3), (0, 3)),
    )
    hurried = (
        ((0, 0), (0, -1), (0, -2), (0, -3), (1, -3)),
        ((0, 0), (0, 1), (0, 2), (1, 2), (1, 3)),
        ((0, 0), (0, 1), (0, 2), (0, -3), (0, -4)),
    )
    patient = (
        ((0, 0), (0, -1), (0, -2), (0, -3), (1, 0), (1, -1)),
        ((0, 0), (0, 1), (0, 2), (1, 0), (1, 1), (1, 2)),
        ((0, 0), None, None, None, (0, -3), (0, -4)),
    )
    moves = ((0, -1), (0, 1), (1, 0))

    def pick(plan, link, step, part):
        if isinstance(step, int):
            return plan[link][step][part]
        found = plan[link][0][part]
        for number in range(1, STEPS):
            found = jnp.where(step == number, plan[link][number][part], found)
        return found

    def sent_shard(plan, link, step):
        return shard(pick(plan, link, step, 0), pick(plan, link, step, 1))

    def got_shard(plan, link, step):
        other, dz = moves[link]
        return shard(pick(plan, link, step, 0) + other, pick(plan, link, step, 1) + dz)

    def used(plan, step, kind):
        if not isinstance(step, int):
            return range(LINKS)
        links = [link for link in range(LINKS) if step < len(plan[link]) and plan[link][step]]
        if plan is hurried and step == STEPS - 1:
            links = [kind]
        return links

    def count(plan, link, kind):
        return sum(link in used(plan, step, kind) for step in range(len(plan[link])))

    def place(kind, lap, index):
        part = pl.ds(pl.multiple_of(index * SLICE, SLICE), SLICE)
        if kind == 0:
            return w_gate.at[lap, part, :]
        if kind == 1:
            return w_first.at[lap, part, :]
        return w_second.at[lap, :, part]

    def own(kind, lap):
        return (gate_ref, first_ref, second_ref)[kind].at[lap]

    def bulk(kind, lap, shards):
        if kind == 0:
            return w_gate.at[lap, pl.ds(0, shards * SLICE), :]
        if kind == 1:
            return w_first.at[lap, pl.ds(0, shards * SLICE), :]
        return w_second.at[lap, :, pl.ds(0, shards * SLICE)]

    def send(plan, lap, step, kind):
        fresh = isinstance(step, int) and step == 0
        for link in used(plan, step, kind):
            index = f if fresh else sent_shard(plan, link, step)
            pltpu.make_async_remote_copy(
                src_ref=own(kind, lap) if fresh else place(kind, lap, index),
                dst_ref=place(kind, lap, index),
                send_sem=gather_send.at[lap, link, kind],
                recv_sem=gather_recv.at[lap, link, step, kind],
                device_id=targets[link],
                device_id_type=MESH,
            ).start()

    def to_twin(lap, kind, index, source):
        pltpu.make_async_remote_copy(
            src_ref=source,
            dst_ref=place(kind, lap, index),
            send_sem=pair_send.at[lap, kind],
            recv_sem=pair_recv.at[lap, kind],
            device_id=twin,
            device_id_type=MESH,
        ).start()

    def keep_own(lap, kind):
        return pltpu.make_async_copy(own(kind, lap), place(kind, lap, f), own_sem.at[lap, kind])

    def gather_begin(lap):
        for kind in range(KINDS):
            send(even, lap, 0, kind)
        for kind in range(KINDS):
            to_twin(lap, kind, f, own(kind, lap))
            keep_own(lap, kind).start()

    def gather_step(plan, lap, step, kind, also=None):
        for link in used(plan, step, kind):
            target = place(kind, lap, got_shard(plan, link, step))
            pltpu.make_async_remote_copy(
                src_ref=target,
                dst_ref=target,
                send_sem=gather_send.at[lap, link, kind],
                recv_sem=gather_recv.at[lap, link, step, kind],
                device_id=targets[link],
                device_id_type=MESH,
            ).wait_recv()
        if isinstance(step, int):
            send(plan, lap, step + 1, kind)
        else:
            pl.when(step + 1 < STEPS)(functools.partial(send, plan, lap, step + 1, kind))
        if also is not None:
            also()
        for link in used(plan, step, kind):
            index = got_shard(plan, link, step)
            to_twin(lap, kind, index, place(kind, lap, index))

    def seat_of(stage, number, kind):
        if kind < 2:
            return passing.at[stage, number, kind]
        return passing_second.at[stage, number]

    def relay(stage, number, kind):
        index = shard(0, -1 - number)
        if stage == 0:
            source, target, device = place(kind, 0, index), seat_of(0, number, kind), mate
        elif stage == 1:
            source, target, device = seat_of(0, number, kind), seat_of(1, number, kind), across
        else:
            source, target, device = seat_of(1, number, kind), place(kind, 0, index), mate
        return pltpu.make_async_remote_copy(
            src_ref=source,
            dst_ref=target,
            send_sem=relay_send.at[stage, number, kind],
            recv_sem=relay_recv.at[stage, number, kind],
            device_id=device,
            device_id_type=MESH,
        )

    def pass_on(stage, number, kind):
        relay(stage, number, kind).wait_recv()
        relay(stage + 1, number, kind).start()

    def gather_end(lap, kind):
        whole = bulk(kind, lap, 16)
        pltpu.make_async_remote_copy(
            src_ref=whole,
            dst_ref=whole,
            send_sem=pair_send.at[lap, kind],
            recv_sem=pair_recv.at[lap, kind],
            device_id=twin,
            device_id_type=MESH,
        ).wait_recv()
        keep_own(lap, kind).wait()

    def gather_drain(plan, lap):
        for kind in range(KINDS):
            for link in range(LINKS):
                part = bulk(kind, lap, count(plan, link, kind))
                pltpu.make_async_remote_copy(
                    src_ref=part,
                    dst_ref=part,
                    send_sem=gather_send.at[lap, link, kind],
                    recv_sem=gather_recv.at[lap, link, 0, kind],
                    device_id=targets[link],
                    device_id_type=MESH,
                ).wait_send()
            whole = bulk(kind, lap, 16)
            pltpu.make_async_remote_copy(
                src_ref=whole,
                dst_ref=whole,
                send_sem=pair_send.at[lap, kind],
                recv_sem=pair_recv.at[lap, kind],
                device_id=twin,
                device_id_type=MESH,
            ).wait_send()

    gather_begin(0)

    def columns(chunk):
        return pl.ds(chunk * CW, CW)

    base = jnp.where(core == 1, MOVED, 0)
    groups = jnp.where(core == 1, MOST, GROUPS - MOVED)

    @pl.when(p == 0)
    def _():
        stage = pltpu.make_async_copy(inputs_ref, staged, stage_sem)
        stage.start()
        stage.wait()
        for pair in range(MB // 2):
            even = staged[plan_ref[2 * pair]].astype(jnp.float32)
            odd = staged[plan_ref[2 * pair + 1]].astype(jnp.float32)
            ordered[3 * pair] = even[:16].astype(jnp.bfloat16)
            ordered[3 * pair + 1] = jnp.concatenate([even[16:], odd[:8]], axis=0).astype(
                jnp.bfloat16
            )
            ordered[3 * pair + 2] = odd[8:].astype(jnp.bfloat16)

    def fill(number, chunk):
        return pltpu.make_async_copy(
            ordered.at[number, :, columns(chunk)],
            xbuf.at[0, base + number, :, columns(chunk)],
            x_recv.at[0, base + number, chunk],
        )

    def over(number, chunk):
        return pltpu.make_async_remote_copy(
            src_ref=ordered.at[GROUPS - MOVED + number, :, columns(chunk)],
            dst_ref=xbuf.at[0, number, :, columns(chunk)],
            send_sem=over_send.at[number, chunk],
            recv_sem=x_recv.at[0, number, chunk],
            device_id=twin,
            device_id_type=MESH,
        )

    def fill_all(number, carry):
        for chunk in range(CHUNKS):
            fill(number, chunk).start()
        return carry

    @pl.when(p == 0)
    def _():
        @pl.when(core == 0)
        def _():
            for number in range(MOVED):
                for chunk in range(CHUNKS):
                    over(number, chunk).start()

        lax.fori_loop(0, jnp.where(core == 1, GROUPS, GROUPS - MOVED), fill_all, 0)

    hurry = p < PIPE // 2

    @pl.when(hurry)
    def _():
        for step in range(STEPS):
            for kind in range(KINDS):
                if step < RELAYED:
                    gather_step(hurried, 0, step, kind, relay(0, step, kind).start)
                else:
                    gather_step(hurried, 0, step, kind)
            if step == STEPS - 2:
                gather_begin(1)
        for number in range(RELAYED):
            for kind in range(KINDS):
                index = shard(1, -1 - number)
                target = place(kind, 0, index)
                pltpu.make_async_remote_copy(
                    src_ref=target,
                    dst_ref=target,
                    send_sem=relay_send.at[2, number, kind],
                    recv_sem=relay_recv.at[2, number, kind],
                    device_id=mate,
                    device_id_type=MESH,
                ).wait_recv()
                to_twin(0, kind, index, target)

    @pl.when(jnp.logical_not(hurry))
    def _():
        last = len(patient[0])
        for step in range(last):
            for kind in range(KINDS):
                for number in range(RELAYED):
                    if step == number + 2:
                        pass_on(1, number, kind)
                    if step == number + 1:
                        pass_on(0, number, kind)
                gather_step(patient, 0, step, kind)
            if step == last - 2:
                gather_begin(1)

    for kind in range(KINDS - 1):
        gather_end(0, kind)

    def next_lap(number, carry):
        for kind in range(KINDS):
            @pl.when(number % KINDS == kind)
            def _():
                gather_step(even, 1, number // KINDS, kind)

        return carry

    early = EARLY * p - jnp.where(hurry, 0, LATER)
    lax.fori_loop(0, early, next_lap, 0)

    onward = ((p + 1) % PIPE, f)
    crossing = (p % 4) == 3

    def hop(lap, group, chunk, to_lap, device):
        return pltpu.make_async_remote_copy(
            src_ref=xbuf.at[lap, group, :, columns(chunk)],
            dst_ref=xbuf.at[to_lap, group, :, columns(chunk)],
            send_sem=x_send.at[lap, group],
            recv_sem=x_recv.at[to_lap, group, chunk],
            device_id=device,
            device_id_type=MESH,
        )

    def finish(group, number, second, slot, index):
        if second:
            seat = 0
        else:
            seat = jnp.where(number % 3 == 0, 0, 1)
        return pltpu.make_async_remote_copy(
            src_ref=xbuf.at[1, group],
            dst_ref=landing.at[seat],
            send_sem=end_send.at[second, group],
            recv_sem=end_recv.at[seat],
            device_id=(slot, index),
            device_id_type=MESH,
        )

    def ends(group):
        moved = (core == 1) & (group < MOVED)
        number = jnp.where(moved, GROUPS - MOVED + group, group - base)
        index = jnp.where(moved, other, f)
        pair = number // 3
        first = 2 * pair + jnp.where(number % 3 == 2, 1, 0)
        leave = moved | (number < GROUPS - 1)
        leave_too = (number % 3 == 1) & (moved | (number < GROUPS - 2))
        return number, index, first, 2 * pair + 1, leave, leave_too

    def one(turn, carry):
        lap = jnp.where(turn >= groups, 1, 0)
        group = turn - lap * groups
        step = early + turn - 1

        @pl.when((turn > 0) & (turn < groups) & (step < ROUNDS))
        def _():
            next_lap(step, 0)

        @pl.when(turn == groups)
        def _():
            lax.fori_loop(jnp.minimum(step, ROUNDS), ROUNDS, next_lap, 0)
            for kind in range(KINDS):
                gather_end(1, kind)

        total_gate = jnp.zeros((GROUP, H), jnp.float32)
        total_first = jnp.zeros((GROUP, H), jnp.float32)
        squares = jnp.zeros((GROUP, 1), jnp.float32)
        for chunk in range(CHUNKS):
            hop(lap, group, chunk, lap, onward).wait_recv()
            wide = xbuf[lap, group, :, columns(chunk)].astype(jnp.float32)
            squares += jnp.sum(wide * wide, axis=-1, keepdims=True)
            scaled = (wide * gains_ref[pl.ds(lap, 1), columns(chunk)]).astype(jnp.bfloat16)
            total_gate += jnp.dot(
                scaled, w_gate[lap, columns(chunk), :], preferred_element_type=jnp.float32
            )
            total_first += jnp.dot(
                scaled, w_first[lap, columns(chunk), :], preferred_element_type=jnp.float32
            )
        scale = lax.rsqrt(squares * (1.0 / D) + EPS)
        gate = total_gate * scale
        hidden = (gate / (1.0 + jnp.exp(-gate)) * (total_first * scale)).astype(jnp.bfloat16)

        @pl.when(turn == 0)
        def _():
            gather_end(0, KINDS - 1)

        last = (p == PIPE - 1) & (lap == 1)
        to_lap = jnp.where(p == PIPE - 1, 1, lap)
        target = (after, jnp.where(crossing & (lap == 0), shard(1, 0), f))

        def down(chunk):
            wide = xbuf[lap, group, :, columns(chunk)].astype(jnp.float32)
            wide += jnp.dot(
                hidden, w_second[lap, :, columns(chunk)], preferred_element_type=jnp.float32
            )
            xbuf[lap, group, :, columns(chunk)] = wide.astype(jnp.bfloat16)

        @pl.when(jnp.logical_not(last))
        def _():
            for chunk in range(CHUNKS):
                down(chunk)
                hop(lap, group, chunk, to_lap, target).start()

        @pl.when(last)
        def _():
            for chunk in range(CHUNKS):
                down(chunk)

        number, index, slot, next_slot, leave, leave_too = ends(group)

        @pl.when(last & leave)
        def _():
            finish(group, number, 0, slot, index).start()

        @pl.when(last & leave_too)
        def _():
            finish(group, number, 1, next_slot, index).start()

        return carry

    lax.fori_loop(0, LAPS * groups, one, 0)

    def put(head, tail):
        head, tail = head.astype(jnp.float32), tail.astype(jnp.float32)

        @pl.when(p % 2 == 0)
        def _():
            o_ref[0] = jnp.concatenate([head, tail[:8]], axis=0).astype(jnp.bfloat16)

        @pl.when(p % 2 == 1)
        def _():
            o_ref[0] = jnp.concatenate([head[8:], tail], axis=0).astype(jnp.bfloat16)

    at_hand = (p == PIPE - 1) & (core == 1)

    @pl.when(jnp.logical_not(at_hand))
    def _():
        for seat in range(2):
            pltpu.make_async_remote_copy(
                src_ref=landing.at[seat],
                dst_ref=landing.at[seat],
                send_sem=end_send.at[0, 0],
                recv_sem=end_recv.at[seat],
                device_id=onward,
                device_id_type=MESH,
            ).wait_recv()
        put(landing[0], landing[1])

    @pl.when(at_hand)
    def _():
        put(xbuf[1, MOST - 2], xbuf[1, MOST - 1])

    @pl.when((p == 0) & (core == 0))
    def _():
        for number in range(MOVED):
            for chunk in range(CHUNKS):
                over(number, chunk).wait_send()

    @pl.when(hurry)
    def _():
        gather_drain(hurried, 0)
        for number in range(RELAYED):
            for kind in range(KINDS):
                relay(0, number, kind).wait_send()

    @pl.when(jnp.logical_not(hurry))
    def _():
        gather_drain(patient, 0)
        for number in range(RELAYED):
            for kind in range(KINDS):
                relay(1, number, kind).wait_send()
                relay(2, number, kind).wait_send()

    gather_drain(even, 1)

    def sent(turn, carry):
        lap = jnp.where(turn >= groups, 1, 0)
        group = turn - lap * groups
        last = (p == PIPE - 1) & (lap == 1)

        @pl.when(jnp.logical_not(last))
        def _():
            pltpu.make_async_remote_copy(
                src_ref=xbuf.at[lap, group],
                dst_ref=xbuf.at[lap, group],
                send_sem=x_send.at[lap, group],
                recv_sem=x_recv.at[lap, group, 0],
                device_id=onward,
                device_id_type=MESH,
            ).wait_send()

        number, index, slot, next_slot, leave, leave_too = ends(group)

        @pl.when(last & leave)
        def _():
            finish(group, number, 0, slot, index).wait_send()

        @pl.when(last & leave_too)
        def _():
            finish(group, number, 1, next_slot, index).wait_send()

        return carry

    lax.fori_loop(0, LAPS * groups, sent, 0)


def local(inputs, gains, proj_gate, proj_in, proj_out, plan):
    anywhere = pl.BlockSpec(memory_space=pl.ANY)
    vmem = pl.BlockSpec(memory_space=pltpu.VMEM)
    dma = pltpu.SemaphoreType.DMA
    rows = MB * TOK
    return pl.pallas_call(
        kernel,
        out_shape=jax.ShapeDtypeStruct((1, TOK, D), jnp.bfloat16),
        in_specs=[
            pl.BlockSpec(memory_space=pltpu.SMEM),
            anywhere,
            vmem,
            anywhere,
            anywhere,
            anywhere,
        ],
        out_specs=vmem,
        scratch_shapes=[
            pltpu.VMEM((LAPS, D, H), jnp.bfloat16),
            pltpu.VMEM((LAPS, D, H), jnp.bfloat16),
            pltpu.VMEM((LAPS, H, D), jnp.bfloat16),
            pltpu.VMEM((MB, TOK, D), jnp.bfloat16),
            pltpu.VMEM((GROUPS, GROUP, D), jnp.bfloat16),
            pltpu.VMEM((LAPS, MOST, GROUP, D), jnp.bfloat16),
            pltpu.VMEM((2, GROUP, D), jnp.bfloat16),
            pltpu.VMEM((2, RELAYED, 2, SLICE, H), jnp.bfloat16),
            pltpu.VMEM((2, RELAYED, H, SLICE), jnp.bfloat16),
            dma,
            dma((LAPS, KINDS)),
            dma((LAPS, LINKS, KINDS)),
            dma((LAPS, LINKS, STEPS + 1, KINDS)),
            dma((LAPS, KINDS)),
            dma((LAPS, KINDS)),
            dma((LAPS, MOST)),
            dma((LAPS, MOST, CHUNKS)),
            dma((2, MOST)),
            dma((2,)),
            dma((MOVED, CHUNKS)),
            dma((3, RELAYED, KINDS)),
            dma((3, RELAYED, KINDS)),
        ],
        compiler_params=pltpu.CompilerParams(
            collective_id=0, has_side_effects=True, vmem_limit_bytes=56 << 20
        ),
        cost_estimate=pl.CostEstimate(
            flops=LAPS * rows * D * H * 6, bytes_accessed=LAPS * D * H * 6, transcendentals=0
        ),
        name="sections",
    )(plan, inputs, gains, proj_gate, proj_in, proj_out)


def solution(mesh):
    in_specs = (
        P(None, "fsdp", None),
        P("pipe", None),
        P("pipe", "fsdp", None),
        P("pipe", "fsdp", None),
        P("pipe", None, "fsdp"),
        P(),
    )
    out_specs = P("pipe", "fsdp", None)
    return jax.shard_map(local, mesh=mesh, in_specs=in_specs, out_specs=out_specs, check_vma=False)
```

```python
import functools

import jax
import jax.numpy as jnp
from jax import lax
from jax.experimental import pallas as pl
from jax.experimental.pallas import tpu as pltpu
from jax.sharding import PartitionSpec as P

MESH = pl.DeviceIdType.MESH
PIPE, FSDP, ZN = 8, 32, 8
D, H, SLICE = 4096, 512, 128
LAPS, MB, TOK = 2, 8, 24
GROUP = 16
GROUPS = MB * TOK // GROUP
MOVED = 2
MOST = GROUPS + MOVED
CHUNKS = 8
CW = D // CHUNKS
WAITS = 4
PER = CHUNKS // WAITS
STEPS, LINKS, KINDS = 5, 3, 3
ROUNDS = STEPS * KINDS
EARLY = 2
LATER = 6
RELAYED = 2
EPS = 1e-05


def kernel(
    plan_ref,
    inputs_ref,
    gains_ref,
    gate_ref,
    first_ref,
    second_ref,
    o_ref,
    w_gate,
    w_first,
    w_second,
    staged,
    ordered,
    xbuf,
    landing,
    passing,
    passing_second,
    stage_sem,
    own_sem,
    gather_send,
    gather_recv,
    pair_send,
    pair_recv,
    x_send,
    x_recv,
    end_send,
    end_recv,
    over_send,
    relay_send,
    relay_recv,
):
    p = lax.axis_index("pipe")
    f = lax.axis_index("fsdp")
    y = f // 16
    z = (f // 2) % ZN
    core = f % 2

    def shard(other, dz):
        row = (y + other) % 2
        return row * 16 + ((z + dz + ZN) % ZN) * 2 + core

    up, down, across = (p, shard(0, 1)), (p, shard(0, -1)), (p, shard(1, 0))
    twin = (p, f + 1 - 2 * core)
    targets = (up, down, across)

    barrier = pltpu.get_barrier_semaphore()
    def greet(device):
        pl.semaphore_signal(barrier, inc=1, device_id=device, device_id_type=MESH)

    other = twin[1]
    before, after = (p + PIPE - 1) % PIPE, (p + 1) % PIPE
    for device in (up, down, across, twin):
        greet(device)
    mate = ((p + PIPE // 2) % PIPE, shard(1, 0))
    greet(mate)
    for section in (before, after):
        greet((section, f))
        greet((section, shard(1, 0)))

    @pl.when(p == PIPE - 1)
    def _():
        for section in range(PIPE - 1):
            greet((section, other))
            if 0 < section < PIPE - 2:
                greet((section, f))

    @pl.when(p < PIPE - 1)
    def _():
        greet((PIPE - 1, other))

    @pl.when((p > 0) & (p < PIPE - 2))
    def _():
        greet((PIPE - 1, f))

    @pl.when(p == PIPE - 1)
    def _():
        pl.semaphore_wait(barrier, 9 + 2 * PIPE - 4)

    @pl.when((p > 0) & (p < PIPE - 2))
    def _():
        pl.semaphore_wait(barrier, 9 + 2)

    @pl.when((p == 0) | (p == PIPE - 2))
    def _():
        pl.semaphore_wait(barrier, 9 + 1)

    even = (
        ((0, 0), (0, -1), (0, -2), (0, -3), (1, -3)),
        ((0, 0), (0, 1), (0, 2), (1, 0), (1, 1)),
        ((0, 0), (0, -1), (0, -2), (0, -3), (0, 3)),
    )
    hurried = (
        ((0, 0), (0, -1), (0, -2), (0, -3), (1, -3)),
        ((0, 0), (0, 1), (0, 2), (1, 2), (1, 3)),
        ((0, 0), (0, 1), (0, 2), (0, -3), (0, -4)),
    )
    patient = (
        ((0, 0), (0, -1), (0, -2), (0, -3), (1, 0), (1, -1)),
        ((0, 0), (0, 1), (0, 2), (1, 0), (1, 1), (1, 2)),
        ((0, 0), None, None, None, (0, -3), (0, -4)),
    )
    moves = ((0, -1), (0, 1), (1, 0))

    def pick(plan, link, step, part):
        if isinstance(step, int):
            return plan[link][step][part]
        found = plan[link][0][part]
        for number in range(1, STEPS):
            found = jnp.where(step == number, plan[link][number][part], found)
        return found

    def sent_shard(plan, link, step):
        return shard(pick(plan, link, step, 0), pick(plan, link, step, 1))

    def got_shard(plan, link, step):
        other, dz = moves[link]
        return shard(pick(plan, link, step, 0) + other, pick(plan, link, step, 1) + dz)

    def used(plan, step, kind):
        if not isinstance(step, int):
            return range(LINKS)
        links = [link for link in range(LINKS) if step < len(plan[link]) and plan[link][step]]
        if plan is hurried and step == STEPS - 1:
            links = [kind]
        return links

    def count(plan, link, kind):
        return sum(link in used(plan, step, kind) for step in range(len(plan[link])))

    def place(kind, lap, index):
        part = pl.ds(pl.multiple_of(index * SLICE, SLICE), SLICE)
        if kind == 0:
            return w_gate.at[lap, part, :]
        if kind == 1:
            return w_first.at[lap, part, :]
        return w_second.at[lap, :, part]

    def own(kind, lap):
        return (gate_ref, first_ref, second_ref)[kind].at[lap]

    def bulk(kind, lap, shards):
        if kind == 0:
            return w_gate.at[lap, pl.ds(0, shards * SLICE), :]
        if kind == 1:
            return w_first.at[lap, pl.ds(0, shards * SLICE), :]
        return w_second.at[lap, :, pl.ds(0, shards * SLICE)]

    def send(plan, lap, step, kind):
        fresh = isinstance(step, int) and step == 0
        for link in used(plan, step, kind):
            index = f if fresh else sent_shard(plan, link, step)
            pltpu.make_async_remote_copy(
                src_ref=own(kind, lap) if fresh else place(kind, lap, index),
                dst_ref=place(kind, lap, index),
                send_sem=gather_send.at[lap, link, kind],
                recv_sem=gather_recv.at[lap, link, step, kind],
                device_id=targets[link],
                device_id_type=MESH,
            ).start()

    def to_twin(lap, kind, index, source):
        pltpu.make_async_remote_copy(
            src_ref=source,
            dst_ref=place(kind, lap, index),
            send_sem=pair_send.at[lap, kind],
            recv_sem=pair_recv.at[lap, kind],
            device_id=twin,
            device_id_type=MESH,
        ).start()

    def keep_own(lap, kind):
        return pltpu.make_async_copy(own(kind, lap), place(kind, lap, f), own_sem.at[lap, kind])

    def gather_begin(lap):
        for kind in range(KINDS):
            send(even, lap, 0, kind)
        for kind in range(KINDS):
            to_twin(lap, kind, f, own(kind, lap))
            keep_own(lap, kind).start()

    def gather_step(plan, lap, step, kind, also=None):
        for link in used(plan, step, kind):
            target = place(kind, lap, got_shard(plan, link, step))
            pltpu.make_async_remote_copy(
                src_ref=target,
                dst_ref=target,
                send_sem=gather_send.at[lap, link, kind],
                recv_sem=gather_recv.at[lap, link, step, kind],
                device_id=targets[link],
                device_id_type=MESH,
            ).wait_recv()
        if isinstance(step, int):
            send(plan, lap, step + 1, kind)
        else:
            pl.when(step + 1 < STEPS)(functools.partial(send, plan, lap, step + 1, kind))
        if also is not None:
            also()
        for link in used(plan, step, kind):
            index = got_shard(plan, link, step)
            to_twin(lap, kind, index, place(kind, lap, index))

    def seat_of(stage, number, kind):
        if kind < 2:
            return passing.at[stage, number, kind]
        return passing_second.at[stage, number]

    def relay(stage, number, kind):
        index = shard(0, -1 - number)
        if stage == 0:
            source, target, device = place(kind, 0, index), seat_of(0, number, kind), mate
        elif stage == 1:
            source, target, device = seat_of(0, number, kind), seat_of(1, number, kind), across
        else:
            source, target, device = seat_of(1, number, kind), place(kind, 0, index), mate
        return pltpu.make_async_remote_copy(
            src_ref=source,
            dst_ref=target,
            send_sem=relay_send.at[stage, number, kind],
            recv_sem=relay_recv.at[stage, number, kind],
            device_id=device,
            device_id_type=MESH,
        )

    def pass_on(stage, number, kind):
        relay(stage, number, kind).wait_recv()
        relay(stage + 1, number, kind).start()

    def gather_end(lap, kind):
        whole = bulk(kind, lap, 16)
        pltpu.make_async_remote_copy(
            src_ref=whole,
            dst_ref=whole,
            send_sem=pair_send.at[lap, kind],
            recv_sem=pair_recv.at[lap, kind],
            device_id=twin,
            device_id_type=MESH,
        ).wait_recv()
        keep_own(lap, kind).wait()

    def gather_drain(plan, lap):
        for kind in range(KINDS):
            for link in range(LINKS):
                part = bulk(kind, lap, count(plan, link, kind))
                pltpu.make_async_remote_copy(
                    src_ref=part,
                    dst_ref=part,
                    send_sem=gather_send.at[lap, link, kind],
                    recv_sem=gather_recv.at[lap, link, 0, kind],
                    device_id=targets[link],
                    device_id_type=MESH,
                ).wait_send()
            whole = bulk(kind, lap, 16)
            pltpu.make_async_remote_copy(
                src_ref=whole,
                dst_ref=whole,
                send_sem=pair_send.at[lap, kind],
                recv_sem=pair_recv.at[lap, kind],
                device_id=twin,
                device_id_type=MESH,
            ).wait_send()

    gather_begin(0)

    def columns(chunk, many=1):
        return pl.ds(chunk * CW, many * CW)

    base = jnp.where(core == 1, MOVED, 0)
    groups = jnp.where(core == 1, MOST, GROUPS - MOVED)

    @pl.when(p == 0)
    def _():
        stage = pltpu.make_async_copy(inputs_ref, staged, stage_sem)
        stage.start()
        stage.wait()
        for pair in range(MB // 2):
            even = staged[plan_ref[2 * pair]].astype(jnp.float32)
            odd = staged[plan_ref[2 * pair + 1]].astype(jnp.float32)
            ordered[3 * pair] = even[:16].astype(jnp.bfloat16)
            ordered[3 * pair + 1] = jnp.concatenate([even[16:], odd[:8]], axis=0).astype(
                jnp.bfloat16
            )
            ordered[3 * pair + 2] = odd[8:].astype(jnp.bfloat16)

    def fill(number, chunk):
        return pltpu.make_async_copy(
            ordered.at[number, :, columns(chunk)],
            xbuf.at[0, base + number, :, columns(chunk)],
            x_recv.at[0, base + number, chunk // PER],
        )

    def over(number, chunk):
        return pltpu.make_async_remote_copy(
            src_ref=ordered.at[GROUPS - MOVED + number, :, columns(chunk)],
            dst_ref=xbuf.at[0, number, :, columns(chunk)],
            send_sem=over_send.at[number, chunk],
            recv_sem=x_recv.at[0, number, chunk // PER],
            device_id=twin,
            device_id_type=MESH,
        )

    def fill_all(number, carry):
        for chunk in range(CHUNKS):
            fill(number, chunk).start()
        return carry

    hurry = p < PIPE // 2

    def fill_some(step):
        part = GROUPS // 3
        most = jnp.where(core == 1, GROUPS, GROUPS - MOVED)

        @pl.when(p == 0)
        def _():
            if step == 0:

                @pl.when(core == 0)
                def _():
                    for number in range(MOVED):
                        for chunk in range(CHUNKS):
                            over(number, chunk).start()

            lax.fori_loop(step * part, jnp.minimum((step + 1) * part, most), fill_all, 0)

    @pl.when(hurry)
    def _():
        for step in range(STEPS):
            for kind in range(KINDS):
                if step < RELAYED:
                    gather_step(hurried, 0, step, kind, relay(0, step, kind).start)
                else:
                    gather_step(hurried, 0, step, kind)
            if step < 3:
                fill_some(step)
            if step == STEPS - 2:
                gather_begin(1)
        for number in range(RELAYED):
            for kind in range(KINDS):
                index = shard(1, -1 - number)
                target = place(kind, 0, index)
                pltpu.make_async_remote_copy(
                    src_ref=target,
                    dst_ref=target,
                    send_sem=relay_send.at[2, number, kind],
                    recv_sem=relay_recv.at[2, number, kind],
                    device_id=mate,
                    device_id_type=MESH,
                ).wait_recv()
                to_twin(0, kind, index, target)

    @pl.when(jnp.logical_not(hurry))
    def _():
        last = len(patient[0])
        for step in range(last):
            for kind in range(KINDS):
                for number in range(RELAYED):
                    if step == number + 2:
                        pass_on(1, number, kind)
                    if step == number + 1:
                        pass_on(0, number, kind)
                gather_step(patient, 0, step, kind)
            if step == last - 2:
                gather_begin(1)

    for kind in range(KINDS - 1):
        gather_end(0, kind)

    def next_lap(number, carry):
        for kind in range(KINDS):
            @pl.when(number % KINDS == kind)
            def _():
                gather_step(even, 1, number // KINDS, kind)

        return carry

    early = EARLY * p - jnp.where(hurry, 0, LATER)
    lax.fori_loop(0, early, next_lap, 0)

    onward = ((p + 1) % PIPE, f)
    crossing = (p % 4) == 3

    def hop(lap, group, chunk, to_lap, device):
        return pltpu.make_async_remote_copy(
            src_ref=xbuf.at[lap, group, :, columns(chunk)],
            dst_ref=xbuf.at[to_lap, group, :, columns(chunk)],
            send_sem=x_send.at[lap, group],
            recv_sem=x_recv.at[to_lap, group, chunk // PER],
            device_id=device,
            device_id_type=MESH,
        )

    def finish(group, number, second, slot, index, cut=None):
        cut = pl.ds(0, D) if cut is None else cut
        if second:
            seat = 0
        else:
            seat = jnp.where(number % 3 == 0, 0, 1)
        return pltpu.make_async_remote_copy(
            src_ref=xbuf.at[1, group, :, cut],
            dst_ref=landing.at[seat, :, cut],
            send_sem=end_send.at[second, group],
            recv_sem=end_recv.at[seat],
            device_id=(slot, index),
            device_id_type=MESH,
        )

    def ends(group):
        moved = (core == 1) & (group < MOVED)
        number = jnp.where(moved, GROUPS - MOVED + group, group - base)
        index = jnp.where(moved, other, f)
        pair = number // 3
        first = 2 * pair + jnp.where(number % 3 == 2, 1, 0)
        leave = moved | (number < GROUPS - 1)
        leave_too = (number % 3 == 1) & (moved | (number < GROUPS - 2))
        return number, index, first, 2 * pair + 1, leave, leave_too

    def one(turn, carry):
        lap = jnp.where(turn >= groups, 1, 0)
        group = turn - lap * groups
        step = early + turn - 1

        @pl.when((turn > 0) & (turn < groups) & (step < ROUNDS))
        def _():
            next_lap(step, 0)

        @pl.when(turn == groups)
        def _():
            lax.fori_loop(jnp.minimum(step, ROUNDS), ROUNDS, next_lap, 0)
            for kind in range(KINDS):
                gather_end(1, kind)

        total_gate = jnp.zeros((GROUP, H), jnp.float32)
        total_first = jnp.zeros((GROUP, H), jnp.float32)
        squares = jnp.zeros((GROUP, 1), jnp.float32)
        for part in range(WAITS):
            wide_columns = columns(part * PER, PER)
            arrived = xbuf.at[lap, group, :, wide_columns]
            pltpu.make_async_remote_copy(
                src_ref=arrived,
                dst_ref=arrived,
                send_sem=x_send.at[lap, group],
                recv_sem=x_recv.at[lap, group, part],
                device_id=onward,
                device_id_type=MESH,
            ).wait_recv()
            wide = xbuf[lap, group, :, wide_columns].astype(jnp.float32)
            squares += jnp.sum(wide * wide, axis=-1, keepdims=True)
            scaled = (wide * gains_ref[pl.ds(lap, 1), wide_columns]).astype(jnp.bfloat16)
            total_gate += jnp.dot(
                scaled, w_gate[lap, wide_columns, :], preferred_element_type=jnp.float32
            )
            total_first += jnp.dot(
                scaled, w_first[lap, wide_columns, :], preferred_element_type=jnp.float32
            )
        scale = lax.rsqrt(squares * (1.0 / D) + EPS)
        gate = total_gate * scale
        hidden = (gate / (1.0 + jnp.exp(-gate)) * (total_first * scale)).astype(jnp.bfloat16)

        @pl.when(turn == 0)
        def _():
            gather_end(0, KINDS - 1)

        last = (p == PIPE - 1) & (lap == 1)
        to_lap = jnp.where(p == PIPE - 1, 1, lap)
        target = (after, jnp.where(crossing & (lap == 0), shard(1, 0), f))

        def down(chunk):
            wide = xbuf[lap, group, :, columns(chunk)].astype(jnp.float32)
            wide += jnp.dot(
                hidden, w_second[lap, :, columns(chunk)], preferred_element_type=jnp.float32
            )
            xbuf[lap, group, :, columns(chunk)] = wide.astype(jnp.bfloat16)

        @pl.when(jnp.logical_not(last))
        def _():
            for chunk in range(CHUNKS):
                down(chunk)
                hop(lap, group, chunk, to_lap, target).start()

        @pl.when(last)
        def _():
            number, index, slot, next_slot, leave, leave_too = ends(group)
            for chunk in range(CHUNKS):
                down(chunk)
                if chunk % 2 == 1:
                    cut = columns(chunk - 1, 2)

                    @pl.when(leave)
                    def _():
                        finish(group, number, 0, slot, index, cut).start()

                    @pl.when(leave_too)
                    def _():
                        finish(group, number, 1, next_slot, index, cut).start()

        return carry

    lax.fori_loop(0, LAPS * groups, one, 0)

    def put(head, tail):
        head, tail = head.astype(jnp.float32), tail.astype(jnp.float32)

        @pl.when(p % 2 == 0)
        def _():
            o_ref[0] = jnp.concatenate([head, tail[:8]], axis=0).astype(jnp.bfloat16)

        @pl.when(p % 2 == 1)
        def _():
            o_ref[0] = jnp.concatenate([head[8:], tail], axis=0).astype(jnp.bfloat16)

    at_hand = (p == PIPE - 1) & (core == 1)

    @pl.when(jnp.logical_not(at_hand))
    def _():
        for seat in range(2):
            pltpu.make_async_remote_copy(
                src_ref=landing.at[seat],
                dst_ref=landing.at[seat],
                send_sem=end_send.at[0, 0],
                recv_sem=end_recv.at[seat],
                device_id=onward,
                device_id_type=MESH,
            ).wait_recv()
        put(landing[0], landing[1])

    @pl.when(at_hand)
    def _():
        put(xbuf[1, MOST - 2], xbuf[1, MOST - 1])

    @pl.when((p == 0) & (core == 0))
    def _():
        for number in range(MOVED):
            for chunk in range(CHUNKS):
                over(number, chunk).wait_send()

    @pl.when(hurry)
    def _():
        gather_drain(hurried, 0)
        for number in range(RELAYED):
            for kind in range(KINDS):
                relay(0, number, kind).wait_send()

    @pl.when(jnp.logical_not(hurry))
    def _():
        gather_drain(patient, 0)
        for number in range(RELAYED):
            for kind in range(KINDS):
                relay(1, number, kind).wait_send()
                relay(2, number, kind).wait_send()

    gather_drain(even, 1)

    def sent(turn, carry):
        lap = jnp.where(turn >= groups, 1, 0)
        group = turn - lap * groups
        last = (p == PIPE - 1) & (lap == 1)

        @pl.when(jnp.logical_not(last))
        def _():
            pltpu.make_async_remote_copy(
                src_ref=xbuf.at[lap, group],
                dst_ref=xbuf.at[lap, group],
                send_sem=x_send.at[lap, group],
                recv_sem=x_recv.at[lap, group, 0],
                device_id=onward,
                device_id_type=MESH,
            ).wait_send()

        number, index, slot, next_slot, leave, leave_too = ends(group)

        @pl.when(last & leave)
        def _():
            finish(group, number, 0, slot, index).wait_send()

        @pl.when(last & leave_too)
        def _():
            finish(group, number, 1, next_slot, index).wait_send()

        return carry

    lax.fori_loop(0, LAPS * groups, sent, 0)


def local(inputs, gains, proj_gate, proj_in, proj_out, plan):
    anywhere = pl.BlockSpec(memory_space=pl.ANY)
    vmem = pl.BlockSpec(memory_space=pltpu.VMEM)
    dma = pltpu.SemaphoreType.DMA
    rows = MB * TOK
    return pl.pallas_call(
        kernel,
        out_shape=jax.ShapeDtypeStruct((1, TOK, D), jnp.bfloat16),
        in_specs=[
            pl.BlockSpec(memory_space=pltpu.SMEM),
            anywhere,
            vmem,
            anywhere,
            anywhere,
            anywhere,
        ],
        out_specs=vmem,
        scratch_shapes=[
            pltpu.VMEM((LAPS, D, H), jnp.bfloat16),
            pltpu.VMEM((LAPS, D, H), jnp.bfloat16),
            pltpu.VMEM((LAPS, H, D), jnp.bfloat16),
            pltpu.VMEM((MB, TOK, D), jnp.bfloat16),
            pltpu.VMEM((GROUPS, GROUP, D), jnp.bfloat16),
            pltpu.VMEM((LAPS, MOST, GROUP, D), jnp.bfloat16),
            pltpu.VMEM((2, GROUP, D), jnp.bfloat16),
            pltpu.VMEM((2, RELAYED, 2, SLICE, H), jnp.bfloat16),
            pltpu.VMEM((2, RELAYED, H, SLICE), jnp.bfloat16),
            dma,
            dma((LAPS, KINDS)),
            dma((LAPS, LINKS, KINDS)),
            dma((LAPS, LINKS, STEPS + 1, KINDS)),
            dma((LAPS, KINDS)),
            dma((LAPS, KINDS)),
            dma((LAPS, MOST)),
            dma((LAPS, MOST, WAITS)),
            dma((2, MOST)),
            dma((2,)),
            dma((MOVED, CHUNKS)),
            dma((3, RELAYED, KINDS)),
            dma((3, RELAYED, KINDS)),
        ],
        compiler_params=pltpu.CompilerParams(
            collective_id=0, has_side_effects=True, vmem_limit_bytes=56 << 20
        ),
        cost_estimate=pl.CostEstimate(
            flops=LAPS * rows * D * H * 6, bytes_accessed=LAPS * D * H * 6, transcendentals=0
        ),
        name="sections",
    )(plan, inputs, gains, proj_gate, proj_in, proj_out)


def solution(mesh):
    in_specs = (
        P(None, "fsdp", None),
        P("pipe", None),
        P("pipe", "fsdp", None),
        P("pipe", "fsdp", None),
        P("pipe", None, "fsdp"),
        P(),
    )
    out_specs = P("pipe", "fsdp", None)
    return jax.shard_map(local, mesh=mesh, in_specs=in_specs, out_specs=out_specs, check_vma=False)
```

```python
import functools

import jax
import jax.numpy as jnp
from jax import lax
from jax.experimental import pallas as pl
from jax.experimental.pallas import tpu as pltpu
from jax.sharding import PartitionSpec as P

MESH = pl.DeviceIdType.MESH
PIPE, FSDP, ZN = 8, 32, 8
D, H, SLICE = 4096, 512, 128
LAPS, MB, TOK = 2, 8, 24
GROUP = 16
GROUPS = MB * TOK // GROUP
MOVED = 2
MOST = GROUPS + MOVED
CHUNKS = 8
CW = D // CHUNKS
WAITS = 4
PER = CHUNKS // WAITS
SENDS = ((0, 1), (1, 1), (2, 2), (4, 2), (6, 2))
STEPS, LINKS, KINDS = 5, 3, 3
ROUNDS = STEPS * KINDS
EARLY = 2
LATER = 6
RELAYED = 2
EPS = 1e-05


def kernel(
    plan_ref,
    inputs_ref,
    gains_ref,
    gate_ref,
    first_ref,
    second_ref,
    o_ref,
    w_gate,
    w_first,
    w_second,
    staged,
    ordered,
    xbuf,
    landing,
    passing,
    passing_second,
    stage_sem,
    own_sem,
    gather_send,
    gather_recv,
    pair_send,
    pair_recv,
    x_send,
    x_recv,
    end_send,
    end_recv,
    over_send,
    relay_send,
    relay_recv,
):
    p = lax.axis_index("pipe")
    f = lax.axis_index("fsdp")
    y = f // 16
    z = (f // 2) % ZN
    core = f % 2

    def shard(other, dz):
        row = (y + other) % 2
        return row * 16 + ((z + dz + ZN) % ZN) * 2 + core

    up, down, across = (p, shard(0, 1)), (p, shard(0, -1)), (p, shard(1, 0))
    twin = (p, f + 1 - 2 * core)
    targets = (up, down, across)

    barrier = pltpu.get_barrier_semaphore()
    def greet(device):
        pl.semaphore_signal(barrier, inc=1, device_id=device, device_id_type=MESH)

    other = twin[1]
    before, after = (p + PIPE - 1) % PIPE, (p + 1) % PIPE
    for device in (up, down, across, twin):
        greet(device)
    mate = ((p + PIPE // 2) % PIPE, shard(1, 0))
    greet(mate)
    for section in (before, after):
        greet((section, f))
        greet((section, shard(1, 0)))

    @pl.when(p == PIPE - 1)
    def _():
        for section in range(PIPE - 1):
            greet((section, other))
            if 0 < section < PIPE - 2:
                greet((section, f))

    @pl.when(p < PIPE - 1)
    def _():
        greet((PIPE - 1, other))

    @pl.when((p > 0) & (p < PIPE - 2))
    def _():
        greet((PIPE - 1, f))

    @pl.when(p == PIPE - 1)
    def _():
        pl.semaphore_wait(barrier, 9 + 2 * PIPE - 4)

    @pl.when((p > 0) & (p < PIPE - 2))
    def _():
        pl.semaphore_wait(barrier, 9 + 2)

    @pl.when((p == 0) | (p == PIPE - 2))
    def _():
        pl.semaphore_wait(barrier, 9 + 1)

    even = (
        ((0, 0), (0, -1), (0, -2), (0, -3), (1, -3)),
        ((0, 0), (0, 1), (0, 2), (1, 0), (1, 1)),
        ((0, 0), (0, -1), (0, -2), (0, -3), (0, 3)),
    )
    hurried = (
        ((0, 0), (0, -1), (0, -2), (0, -3), (1, -3)),
        ((0, 0), (0, 1), (0, 2), (1, 2), (1, 3)),
        ((0, 0), (0, 1), (0, 2), (0, -3), (0, -4)),
    )
    patient = (
        ((0, 0), (0, -1), (0, -2), (0, -3), (1, 0), (1, -1)),
        ((0, 0), (0, 1), (0, 2), (1, 0), (1, 1), (1, 2)),
        ((0, 0), None, None, None, (0, -3), (0, -4)),
    )
    moves = ((0, -1), (0, 1), (1, 0))

    def pick(plan, link, step, part):
        if isinstance(step, int):
            return plan[link][step][part]
        found = plan[link][0][part]
        for number in range(1, STEPS):
            found = jnp.where(step == number, plan[link][number][part], found)
        return found

    def sent_shard(plan, link, step):
        return shard(pick(plan, link, step, 0), pick(plan, link, step, 1))

    def got_shard(plan, link, step):
        other, dz = moves[link]
        return shard(pick(plan, link, step, 0) + other, pick(plan, link, step, 1) + dz)

    def used(plan, step, kind):
        if not isinstance(step, int):
            return range(LINKS)
        links = [link for link in range(LINKS) if step < len(plan[link]) and plan[link][step]]
        if plan is hurried and step == STEPS - 1:
            links = [kind]
        return links

    def count(plan, link, kind):
        return sum(link in used(plan, step, kind) for step in range(len(plan[link])))

    def place(kind, lap, index):
        part = pl.ds(pl.multiple_of(index * SLICE, SLICE), SLICE)
        if kind == 0:
            return w_gate.at[lap, part, :]
        if kind == 1:
            return w_first.at[lap, part, :]
        return w_second.at[lap, :, part]

    def own(kind, lap):
        return (gate_ref, first_ref, second_ref)[kind].at[lap]

    def bulk(kind, lap, shards):
        if kind == 0:
            return w_gate.at[lap, pl.ds(0, shards * SLICE), :]
        if kind == 1:
            return w_first.at[lap, pl.ds(0, shards * SLICE), :]
        return w_second.at[lap, :, pl.ds(0, shards * SLICE)]

    def send(plan, lap, step, kind):
        fresh = isinstance(step, int) and step == 0
        for link in used(plan, step, kind):
            index = f if fresh else sent_shard(plan, link, step)
            pltpu.make_async_remote_copy(
                src_ref=own(kind, lap) if fresh else place(kind, lap, index),
                dst_ref=place(kind, lap, index),
                send_sem=gather_send.at[lap, link, kind],
                recv_sem=gather_recv.at[lap, link, step, kind],
                device_id=targets[link],
                device_id_type=MESH,
            ).start()

    def to_twin(lap, kind, index, source):
        pltpu.make_async_remote_copy(
            src_ref=source,
            dst_ref=place(kind, lap, index),
            send_sem=pair_send.at[lap, kind],
            recv_sem=pair_recv.at[lap, kind],
            device_id=twin,
            device_id_type=MESH,
        ).start()

    def keep_own(lap, kind):
        return pltpu.make_async_copy(own(kind, lap), place(kind, lap, f), own_sem.at[lap, kind])

    def gather_begin(lap):
        for kind in range(KINDS):
            send(even, lap, 0, kind)
        for kind in range(KINDS):
            to_twin(lap, kind, f, own(kind, lap))
            keep_own(lap, kind).start()

    def gather_step(plan, lap, step, kind, also=None):
        for link in used(plan, step, kind):
            target = place(kind, lap, got_shard(plan, link, step))
            pltpu.make_async_remote_copy(
                src_ref=target,
                dst_ref=target,
                send_sem=gather_send.at[lap, link, kind],
                recv_sem=gather_recv.at[lap, link, step, kind],
                device_id=targets[link],
                device_id_type=MESH,
            ).wait_recv()
        if isinstance(step, int):
            send(plan, lap, step + 1, kind)
        else:
            pl.when(step + 1 < STEPS)(functools.partial(send, plan, lap, step + 1, kind))
        if also is not None:
            also()
        for link in used(plan, step, kind):
            index = got_shard(plan, link, step)
            to_twin(lap, kind, index, place(kind, lap, index))

    def seat_of(stage, number, kind):
        if kind < 2:
            return passing.at[stage, number, kind]
        return passing_second.at[stage, number]

    def relay(stage, number, kind):
        index = shard(0, -1 - number)
        if stage == 0:
            source, target, device = place(kind, 0, index), seat_of(0, number, kind), mate
        elif stage == 1:
            source, target, device = seat_of(0, number, kind), seat_of(1, number, kind), across
        else:
            source, target, device = seat_of(1, number, kind), place(kind, 0, index), mate
        return pltpu.make_async_remote_copy(
            src_ref=source,
            dst_ref=target,
            send_sem=relay_send.at[stage, number, kind],
            recv_sem=relay_recv.at[stage, number, kind],
            device_id=device,
            device_id_type=MESH,
        )

    def pass_on(stage, number, kind):
        relay(stage, number, kind).wait_recv()
        relay(stage + 1, number, kind).start()

    def gather_end(lap, kind):
        whole = bulk(kind, lap, 16)
        pltpu.make_async_remote_copy(
            src_ref=whole,
            dst_ref=whole,
            send_sem=pair_send.at[lap, kind],
            recv_sem=pair_recv.at[lap, kind],
            device_id=twin,
            device_id_type=MESH,
        ).wait_recv()
        keep_own(lap, kind).wait()

    def gather_drain(plan, lap):
        for kind in range(KINDS):
            for link in range(LINKS):
                part = bulk(kind, lap, count(plan, link, kind))
                pltpu.make_async_remote_copy(
                    src_ref=part,
                    dst_ref=part,
                    send_sem=gather_send.at[lap, link, kind],
                    recv_sem=gather_recv.at[lap, link, 0, kind],
                    device_id=targets[link],
                    device_id_type=MESH,
                ).wait_send()
            whole = bulk(kind, lap, 16)
            pltpu.make_async_remote_copy(
                src_ref=whole,
                dst_ref=whole,
                send_sem=pair_send.at[lap, kind],
                recv_sem=pair_recv.at[lap, kind],
                device_id=twin,
                device_id_type=MESH,
            ).wait_send()

    gather_begin(0)

    def columns(chunk, many=1):
        return pl.ds(chunk * CW, many * CW)

    base = jnp.where(core == 1, MOVED, 0)
    groups = jnp.where(core == 1, MOST, GROUPS - MOVED)

    @pl.when(p == 0)
    def _():
        stage = pltpu.make_async_copy(inputs_ref, staged, stage_sem)
        stage.start()
        stage.wait()
        for pair in range(MB // 2):
            even = staged[plan_ref[2 * pair]].astype(jnp.float32)
            odd = staged[plan_ref[2 * pair + 1]].astype(jnp.float32)
            ordered[3 * pair] = even[:16].astype(jnp.bfloat16)
            ordered[3 * pair + 1] = jnp.concatenate([even[16:], odd[:8]], axis=0).astype(
                jnp.bfloat16
            )
            ordered[3 * pair + 2] = odd[8:].astype(jnp.bfloat16)

    def fill(number, chunk):
        return pltpu.make_async_copy(
            ordered.at[number, :, columns(chunk)],
            xbuf.at[0, base + number, :, columns(chunk)],
            x_recv.at[0, base + number, chunk // PER],
        )

    def over(number, chunk):
        return pltpu.make_async_remote_copy(
            src_ref=ordered.at[GROUPS - MOVED + number, :, columns(chunk)],
            dst_ref=xbuf.at[0, number, :, columns(chunk)],
            send_sem=over_send.at[number, chunk],
            recv_sem=x_recv.at[0, number, chunk // PER],
            device_id=twin,
            device_id_type=MESH,
        )

    def fill_all(number, carry):
        for chunk in range(CHUNKS):
            fill(number, chunk).start()
        return carry

    hurry = p < PIPE // 2

    def fill_some(step):
        part = GROUPS // 3
        most = jnp.where(core == 1, GROUPS, GROUPS - MOVED)

        @pl.when(p == 0)
        def _():
            if step == 0:

                @pl.when(core == 0)
                def _():
                    for number in range(MOVED):
                        for chunk in range(CHUNKS):
                            over(number, chunk).start()

            lax.fori_loop(step * part, jnp.minimum((step + 1) * part, most), fill_all, 0)

    @pl.when(hurry)
    def _():
        for step in range(STEPS):
            for kind in range(KINDS):
                if step < RELAYED:
                    gather_step(hurried, 0, step, kind, relay(0, step, kind).start)
                else:
                    gather_step(hurried, 0, step, kind)
            if step < 3:
                fill_some(step)
            if step == STEPS - 2:
                gather_begin(1)
        for number in range(RELAYED):
            for kind in range(KINDS):
                index = shard(1, -1 - number)
                target = place(kind, 0, index)
                pltpu.make_async_remote_copy(
                    src_ref=target,
                    dst_ref=target,
                    send_sem=relay_send.at[2, number, kind],
                    recv_sem=relay_recv.at[2, number, kind],
                    device_id=mate,
                    device_id_type=MESH,
                ).wait_recv()
                to_twin(0, kind, index, target)

    @pl.when(jnp.logical_not(hurry))
    def _():
        last = len(patient[0])
        for step in range(last):
            for kind in range(KINDS):
                for number in range(RELAYED):
                    if step == number + 2:
                        pass_on(1, number, kind)
                    if step == number + 1:
                        pass_on(0, number, kind)
                gather_step(patient, 0, step, kind)
            if step == last - 2:
                gather_begin(1)

    for kind in range(KINDS - 1):
        gather_end(0, kind)

    def next_lap(number, carry):
        for kind in range(KINDS):
            @pl.when(number % KINDS == kind)
            def _():
                gather_step(even, 1, number // KINDS, kind)

        return carry

    early = EARLY * p - jnp.where(hurry, 0, LATER)
    lax.fori_loop(0, early, next_lap, 0)

    onward = ((p + 1) % PIPE, f)
    crossing = (p % 4) == 3

    def hop(lap, group, chunk, to_lap, device, many=1):
        return pltpu.make_async_remote_copy(
            src_ref=xbuf.at[lap, group, :, columns(chunk, many)],
            dst_ref=xbuf.at[to_lap, group, :, columns(chunk, many)],
            send_sem=x_send.at[lap, group],
            recv_sem=x_recv.at[to_lap, group, chunk // PER],
            device_id=device,
            device_id_type=MESH,
        )

    def finish(group, number, second, slot, index, cut=None):
        cut = pl.ds(0, D) if cut is None else cut
        if second:
            seat = 0
        else:
            seat = jnp.where(number % 3 == 0, 0, 1)
        return pltpu.make_async_remote_copy(
            src_ref=xbuf.at[1, group, :, cut],
            dst_ref=landing.at[seat, :, cut],
            send_sem=end_send.at[second, group],
            recv_sem=end_recv.at[seat],
            device_id=(slot, index),
            device_id_type=MESH,
        )

    def ends(group):
        moved = (core == 1) & (group < MOVED)
        number = jnp.where(moved, GROUPS - MOVED + group, group - base)
        index = jnp.where(moved, other, f)
        pair = number // 3
        first = 2 * pair + jnp.where(number % 3 == 2, 1, 0)
        leave = moved | (number < GROUPS - 1)
        leave_too = (number % 3 == 1) & (moved | (number < GROUPS - 2))
        return number, index, first, 2 * pair + 1, leave, leave_too

    def one(turn, carry):
        lap = jnp.where(turn >= groups, 1, 0)
        group = turn - lap * groups
        step = early + turn - 1

        @pl.when((turn > 0) & (turn < groups) & (step < ROUNDS))
        def _():
            next_lap(step, 0)

        @pl.when(turn == groups)
        def _():
            lax.fori_loop(jnp.minimum(step, ROUNDS), ROUNDS, next_lap, 0)
            for kind in range(KINDS):
                gather_end(1, kind)

        total_gate = jnp.zeros((GROUP, H), jnp.float32)
        total_first = jnp.zeros((GROUP, H), jnp.float32)
        squares = jnp.zeros((GROUP, 1), jnp.float32)
        for part in range(WAITS):
            wide_columns = columns(part * PER, PER)
            arrived = xbuf.at[lap, group, :, wide_columns]
            pltpu.make_async_remote_copy(
                src_ref=arrived,
                dst_ref=arrived,
                send_sem=x_send.at[lap, group],
                recv_sem=x_recv.at[lap, group, part],
                device_id=onward,
                device_id_type=MESH,
            ).wait_recv()
            wide = xbuf[lap, group, :, wide_columns].astype(jnp.float32)
            squares += jnp.sum(wide * wide, axis=-1, keepdims=True)
            scaled = (wide * gains_ref[pl.ds(lap, 1), wide_columns]).astype(jnp.bfloat16)
            total_gate += jnp.dot(
                scaled, w_gate[lap, wide_columns, :], preferred_element_type=jnp.float32
            )
            total_first += jnp.dot(
                scaled, w_first[lap, wide_columns, :], preferred_element_type=jnp.float32
            )
        scale = lax.rsqrt(squares * (1.0 / D) + EPS)
        gate = total_gate * scale
        hidden = (gate / (1.0 + jnp.exp(-gate)) * (total_first * scale)).astype(jnp.bfloat16)

        @pl.when(turn == 0)
        def _():
            gather_end(0, KINDS - 1)

        last = (p == PIPE - 1) & (lap == 1)
        to_lap = jnp.where(p == PIPE - 1, 1, lap)
        target = (after, jnp.where(crossing & (lap == 0), shard(1, 0), f))

        def down(chunk, many=1):
            wide = xbuf[lap, group, :, columns(chunk, many)].astype(jnp.float32)
            wide += jnp.dot(
                hidden, w_second[lap, :, columns(chunk, many)], preferred_element_type=jnp.float32
            )
            xbuf[lap, group, :, columns(chunk, many)] = wide.astype(jnp.bfloat16)

        @pl.when(jnp.logical_not(last))
        def _():
            for chunk, many in SENDS:
                down(chunk, many)
                hop(lap, group, chunk, to_lap, target, many).start()

        @pl.when(last)
        def _():
            number, index, slot, next_slot, leave, leave_too = ends(group)
            for chunk in range(CHUNKS):
                down(chunk)
                if chunk % 2 == 1:
                    cut = columns(chunk - 1, 2)

                    @pl.when(leave)
                    def _():
                        finish(group, number, 0, slot, index, cut).start()

                    @pl.when(leave_too)
                    def _():
                        finish(group, number, 1, next_slot, index, cut).start()

        return carry

    lax.fori_loop(0, LAPS * groups, one, 0)

    def put(head, tail):
        head, tail = head.astype(jnp.float32), tail.astype(jnp.float32)

        @pl.when(p % 2 == 0)
        def _():
            o_ref[0] = jnp.concatenate([head, tail[:8]], axis=0).astype(jnp.bfloat16)

        @pl.when(p % 2 == 1)
        def _():
            o_ref[0] = jnp.concatenate([head[8:], tail], axis=0).astype(jnp.bfloat16)

    at_hand = (p == PIPE - 1) & (core == 1)

    @pl.when(jnp.logical_not(at_hand))
    def _():
        for seat in range(2):
            pltpu.make_async_remote_copy(
                src_ref=landing.at[seat],
                dst_ref=landing.at[seat],
                send_sem=end_send.at[0, 0],
                recv_sem=end_recv.at[seat],
                device_id=onward,
                device_id_type=MESH,
            ).wait_recv()
        put(landing[0], landing[1])

    @pl.when(at_hand)
    def _():
        put(xbuf[1, MOST - 2], xbuf[1, MOST - 1])

    @pl.when((p == 0) & (core == 0))
    def _():
        for number in range(MOVED):
            for chunk in range(CHUNKS):
                over(number, chunk).wait_send()

    @pl.when(hurry)
    def _():
        gather_drain(hurried, 0)
        for number in range(RELAYED):
            for kind in range(KINDS):
                relay(0, number, kind).wait_send()

    @pl.when(jnp.logical_not(hurry))
    def _():
        gather_drain(patient, 0)
        for number in range(RELAYED):
            for kind in range(KINDS):
                relay(1, number, kind).wait_send()
                relay(2, number, kind).wait_send()

    gather_drain(even, 1)

    def sent(turn, carry):
        lap = jnp.where(turn >= groups, 1, 0)
        group = turn - lap * groups
        last = (p == PIPE - 1) & (lap == 1)

        @pl.when(jnp.logical_not(last))
        def _():
            pltpu.make_async_remote_copy(
                src_ref=xbuf.at[lap, group],
                dst_ref=xbuf.at[lap, group],
                send_sem=x_send.at[lap, group],
                recv_sem=x_recv.at[lap, group, 0],
                device_id=onward,
                device_id_type=MESH,
            ).wait_send()

        number, index, slot, next_slot, leave, leave_too = ends(group)

        @pl.when(last & leave)
        def _():
            finish(group, number, 0, slot, index).wait_send()

        @pl.when(last & leave_too)
        def _():
            finish(group, number, 1, next_slot, index).wait_send()

        return carry

    lax.fori_loop(0, LAPS * groups, sent, 0)


def local(inputs, gains, proj_gate, proj_in, proj_out, plan):
    anywhere = pl.BlockSpec(memory_space=pl.ANY)
    vmem = pl.BlockSpec(memory_space=pltpu.VMEM)
    dma = pltpu.SemaphoreType.DMA
    rows = MB * TOK
    return pl.pallas_call(
        kernel,
        out_shape=jax.ShapeDtypeStruct((1, TOK, D), jnp.bfloat16),
        in_specs=[
            pl.BlockSpec(memory_space=pltpu.SMEM),
            anywhere,
            vmem,
            anywhere,
            anywhere,
            anywhere,
        ],
        out_specs=vmem,
        scratch_shapes=[
            pltpu.VMEM((LAPS, D, H), jnp.bfloat16),
            pltpu.VMEM((LAPS, D, H), jnp.bfloat16),
            pltpu.VMEM((LAPS, H, D), jnp.bfloat16),
            pltpu.VMEM((MB, TOK, D), jnp.bfloat16),
            pltpu.VMEM((GROUPS, GROUP, D), jnp.bfloat16),
            pltpu.VMEM((LAPS, MOST, GROUP, D), jnp.bfloat16),
            pltpu.VMEM((2, GROUP, D), jnp.bfloat16),
            pltpu.VMEM((2, RELAYED, 2, SLICE, H), jnp.bfloat16),
            pltpu.VMEM((2, RELAYED, H, SLICE), jnp.bfloat16),
            dma,
            dma((LAPS, KINDS)),
            dma((LAPS, LINKS, KINDS)),
            dma((LAPS, LINKS, STEPS + 1, KINDS)),
            dma((LAPS, KINDS)),
            dma((LAPS, KINDS)),
            dma((LAPS, MOST)),
            dma((LAPS, MOST, WAITS)),
            dma((2, MOST)),
            dma((2,)),
            dma((MOVED, CHUNKS)),
            dma((3, RELAYED, KINDS)),
            dma((3, RELAYED, KINDS)),
        ],
        compiler_params=pltpu.CompilerParams(
            collective_id=0, has_side_effects=True, vmem_limit_bytes=56 << 20
        ),
        cost_estimate=pl.CostEstimate(
            flops=LAPS * rows * D * H * 6, bytes_accessed=LAPS * D * H * 6, transcendentals=0
        ),
        name="sections",
    )(plan, inputs, gains, proj_gate, proj_in, proj_out)


def solution(mesh):
    in_specs = (
        P(None, "fsdp", None),
        P("pipe", None),
        P("pipe", "fsdp", None),
        P("pipe", "fsdp", None),
        P("pipe", None, "fsdp"),
        P(),
    )
    out_specs = P("pipe", "fsdp", None)
    return jax.shard_map(local, mesh=mesh, in_specs=in_specs, out_specs=out_specs, check_vma=False)
```
